128 devices in a mesh: ctx: 8 (over x, core), exp: 16 (over y, z).
Axes of the slice: x: 4, y: 4, z: 4, core: 2. Of those that a mesh axis runs over, the one named last changes fastest.
Arguments:
- hidden_in: bfloat16 [8192, 2048], P(('ctx', 'exp')), may hold values from -6 to 6
- queries: bfloat16 [8192, 2048], P('ctx', 'exp'), may hold values from -72 to 72
- keys: bfloat16 [65536, 2048], P('ctx', 'exp'), may hold values from -6 to 6
- values: bfloat16 [65536, 2048], P('ctx', 'exp'), may hold values from -12 to 12
- block_choice: int32 [16, 8], replicated, may hold values from -1 to 15, as said below
- out_proj: bfloat16 [2048, 2048], P('exp'), may hold values from -0.125 to 0.125
- norm_gain: float32 [2048], replicated, may hold values from 0.1 to 1.9
- router: bfloat16 [2048, 16], replicated, may hold values from -0.25 to 0.25
- expert_ids: int32 [8192, 6], P(('ctx', 'exp')), may hold values from 0 to 15, all different within a row; in each aligned block of 64 rows (0 to 63, 64 to 127, ...) at most 36 rows name the same one
- w_gate: bfloat16 [16, 2048, 1408], P('exp'), may hold values from -0.125 to 0.125
- w_up: bfloat16 [16, 2048, 1408], P('exp'), may hold values from -0.125 to 0.125
- w_down: bfloat16 [16, 1408, 2048], P('exp'), may hold values from -0.15625 to 0.15625
Outputs:
- layer_out: bfloat16 [8192, 2048], P(('ctx', 'exp'))
The draws below stay inside these ranges and needn't reach their ends.
Inputs may be any that keep to these rules, and one draw needn't show every extreme that they name: `block_choice`: row r lists the key blocks chosen by block r: its first entry is r, the others are distinct blocks before r; a row r < 7 holds -1 in its last 7 - r entries. `expert_ids`: each row names 6 different experts; the rows of one device name no expert more than 36 times.
All inputs are finite; a program needn't handle non-finite values.
Results may differ from the reference program's by a relative error of at most 0.02.
Values may be sent and summed in bfloat16 or wider, within the bound.
A program may use at most 192 MiB of HBM per device.

```python
import math
import jax
import jax.numpy as jnp
import numpy as np
from jax import lax

D = 2048
HEADS = 16
HD = 128
FF = 1408
TOPK = 6
BLK = 4096
SEL = 8
NBLK = 16
TOK_DEV = 64
EXPERTS = 16
CAP = 36
S_CTX = 1024
TOKENS = 8192
KVTOK = 65536


def key_base(key):
    raw_normal = jax.random.normal(jax.random.fold_in(key, 11), (KVTOK, HEADS * HD), jnp.float32)
    return jnp.clip(1.5 * raw_normal, -6.0, 6.0)


def draw_keys(key, part):
    base_keys = key_base(key)
    return base_keys.astype(jnp.bfloat16)


def draw_queries(key, part):
    key = jax.random.fold_in(key, 5)
    fresh = jnp.clip(1.5 * jax.random.normal(key, (TOKENS, HEADS * HD), jnp.float32), -6.0, 6.0)
    return fresh.astype(jnp.bfloat16)


def draw_block_choice(key, part):
    key = jax.random.fold_in(key, 7)
    row_index = jnp.arange(NBLK, dtype=jnp.int32)[:, None]
    col_index = jnp.arange(NBLK, dtype=jnp.int32)[None, :]
    random_rank = jax.random.randint(key, (NBLK, NBLK), 0, 1 << 20, dtype=jnp.int32)
    rank_score = jnp.where(col_index < row_index, random_rank * NBLK + col_index, -1)
    top_score, picked = lax.top_k(rank_score, SEL - 1)
    picked = jnp.where(top_score >= 0, picked.astype(jnp.int32), -1)
    own_block = jnp.arange(NBLK, dtype=jnp.int32)[:, None]
    return jnp.concatenate([own_block, picked], axis=1)


def steps_of(key, extent, split, least, largest):
    def one(axis_at, blocks):
        draws = jax.random.uniform(jax.random.fold_in(jax.random.fold_in(key, 6), axis_at), (blocks,), jnp.float32, least / len(split), largest / len(split))
        return jnp.repeat(jnp.exp(draws), extent[axis_at] // blocks).reshape((-1,) + (1,) * (len(extent) - axis_at - 1))

    gain = one(*split[0])
    for cut in split[1:]:
        gain = gain * one(*cut)
    return gain


def shared_out(own_key, own, number, rows, number_of, top, limit, lean):
    ranking = jax.random.permutation(own_key, number_of)
    packed, usual = portions_of(number_of, rows * top, limit, lean, True), portions_of(number_of, rows * top, limit, lean, False)
    places = jnp.arange(number_of)

    def named(tallies, rotation):
        used = int((tallies > 0).sum())
        fixed = max(1, used // 4)
        passed = fixed + (places - fixed + rotation * (used - fixed)) % max(1, number_of - fixed)
        return jnp.zeros((number_of,), jnp.int32).at[ranking[jnp.where(places < fixed, places, passed)]].set(jnp.asarray(tallies, jnp.int32))

    tallies = jnp.where(number % 4 == 0, named(packed, number // 4), named(usual, number - number // 4 - 1))
    mixed = jax.random.permutation(jax.random.fold_in(own, 3), number_of)
    giver, receiver = mixed[0:number_of // 2 * 2:2], mixed[1:number_of // 2 * 2:2]
    room = jnp.minimum(tallies[giver] - 1, limit - tallies[receiver]) // 2
    room = jnp.where((giver == ranking[0]) | (receiver == ranking[0]) | (tallies[receiver] == 0), 0, jnp.maximum(room, 0))
    passed = jax.random.randint(jax.random.fold_in(own, 4), (number_of // 2,), 0, 1 << 20) % (room + 1)
    tallies = tallies.at[giver].add(-passed).at[receiver].add(passed)
    labels = jnp.searchsorted(jnp.cumsum(tallies), jnp.arange(rows * top), side="right").astype(jnp.int32)
    table = labels.reshape(top, rows).T
    table = table[jax.random.permutation(jax.random.fold_in(own, 1), rows)]
    rotation = jax.random.randint(jax.random.fold_in(own, 2), (rows, 1), 0, top)
    return jnp.take_along_axis(table, (jnp.arange(top)[None, :] + rotation) % top, axis=1)


def portions_of(amount, total, bound, skew, full):
    weights = [(1 << 20) // math.isqrt(standing ** skew) + 1 for standing in range(1, amount + 1)]
    largest = bound if full else min(bound, max(-(-total // amount), total * weights[0] // sum(weights)))
    least = 1 if total - largest >= amount - 1 else 0
    holding, surplus = [largest] + [least] * (amount - 1), total - largest - least * (amount - 1)
    while surplus > 0:
        candidates = [i for i in range(1, amount) if holding[i] < largest] or [i for i in range(1, amount) if holding[i] < bound]
        mass, budget = sum([weights[i] for i in candidates]), surplus
        for i in candidates:
            more = min(bound - holding[i], max(1, budget * weights[i] // mass), surplus)
            holding[i] = holding[i] + more
            surplus = surplus - more
    return np.array(holding)


def gaussian(own_key, extent, width, limit, split=(), held_as=jnp.bfloat16):
    values = jax.random.normal(own_key, extent, jnp.float32) * width
    if len(split) > 0:
        values = steps_of(own_key, extent, split, -0.22, 0.18) * values
    return jnp.clip(values, min=-limit, max=limit).astype(held_as)


def setup_inputs(seed: int = 0) -> dict:
    seeds = jax.random.split(jax.random.key(seed), 13)
    hidden_in = gaussian(seeds[0], (TOKENS, D), 1.0, 6.0, ((0, 128),))
    queries = draw_queries(jax.random.fold_in(seeds[12], 71), 0)
    keys = draw_keys(jax.random.fold_in(seeds[12], 71), 0)
    values = gaussian(seeds[3], (KVTOK, HEADS * HD), 3.0, 12.0, ((0, 8), (1, 16)))
    block_choice = draw_block_choice(jax.random.fold_in(seeds[12], 71), 0)
    out_proj = gaussian(seeds[5], (HEADS * HD, D), (HEADS * HD) ** -0.5, 0.125, ((0, 16),))
    norm_gain = jnp.clip(1.0 + 0.18 * jax.random.normal(seeds[6], (D,), jnp.float32), 0.1, 1.9)
    router = gaussian(seeds[7], (D, EXPERTS), (D // 4) ** -0.5, 0.25)
    expert_ids_keys = jax.random.split(jax.random.fold_in(seeds[8], 1), TOKENS // TOK_DEV)
    expert_ids_turns = jax.random.permutation(jax.random.fold_in(seeds[8], 3), TOKENS // TOK_DEV)
    expert_ids = jax.vmap(lambda own, number: shared_out(jax.random.fold_in(seeds[8], 2), own, number, TOK_DEV, EXPERTS, TOPK, CAP, 2))(expert_ids_keys, expert_ids_turns).reshape((TOKENS, TOPK))
    w_gate = gaussian(seeds[9], (EXPERTS, D, FF), D ** -0.5, 0.125, ((0, 16),))
    w_up = gaussian(seeds[10], (EXPERTS, D, FF), D ** -0.5, 0.125, ((0, 16),))
    w_down = gaussian(seeds[11], (EXPERTS, FF, D), FF ** -0.5, 0.15625, ((0, 16),))
    return {"hidden_in": hidden_in, "queries": queries, "keys": keys, "values": values, "block_choice": block_choice, "out_proj": out_proj, "norm_gain": norm_gain, "router": router, "expert_ids": expert_ids, "w_gate": w_gate, "w_up": w_up, "w_down": w_down}


ROUTE_SCALE = 2.446
NORM_EPS = 1e-06

def attend_head(head_queries, head_keys, head_values, block_choice):
    key_blocks = head_keys.reshape(NBLK, BLK, HD)
    value_blocks = head_values.reshape(NBLK, BLK, HD)
    group_count = TOKENS // S_CTX
    query_groups = head_queries.reshape(group_count, S_CTX, HD)
    group_first = (KVTOK - TOKENS + jnp.arange(group_count, dtype=jnp.int32) * S_CTX).astype(jnp.int32)

    def one_group(group_args):
        query_rows, first_pos = group_args
        own_block = (first_pos // BLK).astype(jnp.int32)
        picked = lax.dynamic_index_in_dim(block_choice, own_block, 0, keepdims=False)
        safe_picks = jnp.maximum(picked, 0)
        key_sel = key_blocks[safe_picks].astype(jnp.float32)
        value_sel = value_blocks[safe_picks].astype(jnp.float32)
        scores = jnp.einsum('qd,skd->qsk', query_rows.astype(jnp.float32), key_sel) * HD ** (-0.5)
        query_pos = first_pos + jnp.arange(S_CTX, dtype=jnp.int32)
        key_pos = safe_picks[:, None] * BLK + jnp.arange(BLK, dtype=jnp.int32)[None, :]
        listed = (picked >= 0)[None, :, None]
        foreign = (picked != own_block)[None, :, None]
        allowed = listed & (foreign | (key_pos[None, :, :] <= query_pos[:, None, None]))
        scores = jnp.where(allowed, scores, -jnp.inf)
        row_max = lax.optimization_barrier(jnp.max(scores, axis=(1, 2), keepdims=True))
        exponentials = jnp.exp(scores - row_max)
        denominator = lax.optimization_barrier(jnp.sum(exponentials, axis=(1, 2), keepdims=True))
        probabilities = (exponentials / denominator).astype(jnp.bfloat16)
        mixed = jnp.einsum('qsk,skd->qd', probabilities.astype(jnp.float32), value_sel)
        return mixed.astype(jnp.bfloat16)
    return lax.map(one_group, (query_groups, group_first)).reshape(TOKENS, HD)

def reference(hidden_in, queries, keys, values, block_choice, out_proj, norm_gain, router, expert_ids, w_gate, w_up, w_down):
    head_queries = queries.reshape(TOKENS, HEADS, HD).transpose(1, 0, 2)
    head_keys = keys.reshape(KVTOK, HEADS, HD).transpose(1, 0, 2)
    head_values = values.reshape(KVTOK, HEADS, HD).transpose(1, 0, 2)

    def one_head(head_args):
        return attend_head(head_args[0], head_args[1], head_args[2], block_choice)
    per_head = lax.map(one_head, (head_queries, head_keys, head_values))
    attended = per_head.transpose(1, 0, 2).reshape(TOKENS, HEADS * HD)
    projected = jnp.dot(attended, out_proj, preferred_element_type=jnp.float32)
    residual = (hidden_in.astype(jnp.float32) + projected).astype(jnp.bfloat16)
    residual_wide = residual.astype(jnp.float32)
    mean_square = lax.optimization_barrier(jnp.mean(residual_wide * residual_wide, axis=1, keepdims=True))
    normed = (residual_wide * lax.rsqrt(mean_square + NORM_EPS) * norm_gain.astype(jnp.float32)).astype(jnp.bfloat16)
    affinity = jax.nn.sigmoid(jnp.dot(normed, router, preferred_element_type=jnp.float32))
    picked = jnp.take_along_axis(affinity, expert_ids, axis=1)
    mix_weight = ROUTE_SCALE * picked / lax.optimization_barrier(jnp.sum(picked, axis=1, keepdims=True))
    row_bound = min(TOKENS, TOKENS // TOK_DEV * CAP)

    def add_expert(running, expert_args):
        gate_rows, up_rows, down_rows, expert_index = expert_args
        chosen = expert_ids == expert_index
        share = lax.optimization_barrier(jnp.sum(jnp.where(chosen, mix_weight, 0.0), axis=1))
        hit = jnp.any(chosen, axis=1)
        row_count = jnp.sum(hit.astype(jnp.int32))
        token_index = jnp.nonzero(hit, size=row_bound, fill_value=0)[0].astype(jnp.int32)
        live = jnp.arange(row_bound, dtype=jnp.int32) < row_count
        input_rows = normed[token_index]
        gate_part = jnp.dot(input_rows, gate_rows, preferred_element_type=jnp.float32)
        up_part = jnp.dot(input_rows, up_rows, preferred_element_type=jnp.float32)
        hidden_units = (jax.nn.silu(gate_part) * up_part).astype(jnp.bfloat16)
        expert_out = jnp.dot(hidden_units, down_rows, preferred_element_type=jnp.float32).astype(jnp.bfloat16)
        contribution = jnp.where(live, share[token_index], 0.0)[:, None] * expert_out.astype(jnp.float32)
        return (running.at[token_index].add(contribution), None)
    start_sum = jnp.zeros((TOKENS, D), jnp.float32)
    running, unused = lax.scan(add_expert, start_sum, (w_gate, w_up, w_down, jnp.arange(EXPERTS, dtype=jnp.int32)))
    return (residual_wide + running).astype(jnp.bfloat16)
```

```python
import functools

import jax
import jax.numpy as jnp
from jax import lax
from jax.experimental import pallas as pl
from jax.experimental.pallas import tpu as pltpu
from jax.sharding import PartitionSpec as P

HD = 128
BLK = 4096
ROUTE_SCALE = 2.446
NORM_EPS = 1e-06
LOG2E = 1.4426950408889634
LOW = -1e30
JUMP = 100.0
MESH = pl.DeviceIdType.MESH
MIB = 2**20

CHUNK = 1024
TQ = 512
SUB = 128
TKS = 1024
CHIPS = 4
SLOTS = 4
CAP = 36
TOK = 64
EXPERTS = 16
GROUP = EXPERTS * TOK


def nt(a, b):
    return lax.dot_general(a, b, (((1,), (1,)), ((), ())), preferred_element_type=jnp.float32)


def mm(a, b):
    return jnp.dot(a, b, preferred_element_type=jnp.float32)


def attention_kernel(
    choice, q_ref, k_own, k_oth, v_own, v_oth, o_ref, lse_ref,
    k_all, v_all, acc, m_s, l_s, r_s, mx_s, fresh, sems,
):
    scale = HD**-0.5 * LOG2E
    ctx = lax.axis_index("ctx")
    core = lax.rem(ctx, 2)
    other = ctx + 1 - 2 * core
    copies = []
    for slot in range(SLOTS):
        src_k, src_v = (k_own, v_own) if slot < 2 else (k_oth, v_oth)
        src = pl.ds((slot % 2) * BLK, BLK)
        dst = pl.ds(slot * BLK, BLK)
        copies.append(
            (
                pltpu.make_async_copy(src_k.at[src], k_all.at[dst], sems.at[0, slot]),
                pltpu.make_async_copy(src_v.at[src], v_all.at[dst], sems.at[1, slot]),
            )
        )
    for pair in copies:
        for copy in pair:
            copy.start()
    for pair in copies:
        for copy in pair:
            copy.wait()
    ones = jnp.ones((BLK, HD), jnp.bfloat16)

    def careful(q0, slot, steps, reach):
        @pl.loop(0, steps)
        def _(step):
            at = pl.ds(pl.multiple_of(slot * BLK + step * TKS, TKS), TKS)
            keys = k_all[at, :]
            vals = v_all[at, :]
            for i in range(TQ // SUB):
                rows = pl.ds(i * SUB, SUB)
                q = q_ref[pl.ds(pl.multiple_of(q0 + i * SUB, SUB), SUB), :]
                s = nt(q, keys) * scale
                key_pos = step * TKS + lax.broadcasted_iota(jnp.int32, (SUB, TKS), 1)
                query_pos = reach + i * SUB + lax.broadcasted_iota(jnp.int32, (SUB, TKS), 0)
                s = jnp.where(key_pos <= query_pos, s, LOW)
                old = m_s[rows]
                new = jnp.maximum(old, jnp.max(s, axis=1, keepdims=True))
                fade = jnp.exp2(old - new)
                p = jnp.exp2(s - new[:, :1])
                m_s[rows] = new
                l_s[rows] = l_s[rows] * fade + jnp.sum(p, axis=1, keepdims=True)
                acc[rows] = acc[rows] * fade + mm(p.astype(jnp.bfloat16), vals)

    def quick(q0, slot):
        base = pl.multiple_of(slot * BLK, BLK)
        keys = k_all[pl.ds(base, BLK), :]
        vals = jnp.concatenate([v_all[pl.ds(base, BLK), :], ones], axis=1)

        @pl.when(fresh[0] == 1)
        def _():
            some = k_all[pl.ds(base, 256), :]
            s = nt(q_ref[pl.ds(q0, TQ), :], some) * scale
            m_s[...] = jnp.broadcast_to(jnp.max(s, axis=1, keepdims=True), m_s.shape)

        for i in range(TQ // SUB):
            rows = pl.ds(i * SUB, SUB)
            q = q_ref[pl.ds(pl.multiple_of(q0 + i * SUB, SUB), SUB), :]
            s = nt(q, keys)
            old = m_s[rows]
            mx_s[rows] = jnp.broadcast_to(jnp.max(s, axis=1, keepdims=True) * scale, old.shape)
            p = jnp.exp2(s * scale - old[:, :1])
            r_s[rows] = mm(p.astype(jnp.bfloat16), vals)
        jump = jnp.max(mx_s[...] - m_s[...])

        @pl.when(jump <= JUMP)
        def _():
            old = m_s[...]
            new = jnp.maximum(old, mx_s[...])
            fade = jnp.exp2(old - new)
            m_s[...] = new
            acc[...] = (acc[...] + r_s[:, :HD]) * fade
            l_s[...] = (l_s[...] + r_s[:, HD:]) * fade

        @pl.when(jnp.logical_not(jump <= JUMP))
        def _():
            careful(q0, slot, BLK // TKS, BLK)

    @pl.loop(0, CHIPS * CHUNK // TQ)
    def _(tile):
        q0 = pl.multiple_of(tile * TQ, TQ)
        chunk = tile // (CHUNK // TQ)
        row = 14 + chunk // 2
        in_block = lax.rem(2 * chunk + core, 4) * CHUNK + lax.rem(tile, CHUNK // TQ) * TQ
        acc[...] = jnp.zeros_like(acc)
        l_s[...] = jnp.zeros_like(l_s)
        m_s[...] = jnp.full_like(m_s, LOW)
        fresh[0] = 1

        @pl.loop(0, SLOTS)
        def _(slot):
            block = jnp.where(slot < 2, 2 * ctx + slot, 2 * other + slot - 2)
            hit = choice[row, 1] == block
            for j in range(2, 8):
                hit = jnp.logical_or(hit, choice[row, j] == block)
            own = block == row

            @pl.when(own)
            def _():
                careful(q0, slot, in_block // TKS + 1, in_block)
                fresh[0] = 0

            @pl.when(jnp.logical_and(hit, jnp.logical_not(own)))
            def _():
                quick(q0, slot)
                fresh[0] = 0

        total = l_s[...]
        some = total > 0.0
        total = jnp.where(some, total, 1.0)
        o_ref[pl.ds(q0, TQ), :] = (acc[...] / total).astype(jnp.bfloat16)
        lse = jnp.where(some, m_s[...] + jnp.log2(total), LOW)
        flat = jnp.transpose(lse)
        for i in range(TQ // HD):
            lse_ref[pl.ds(tile * (TQ // HD) + i, 1), :] = flat[:1, i * HD : (i + 1) * HD]


def attend(choice, q_all, k_own, k_oth, v_own, v_oth):
    rows = CHIPS * CHUNK
    anywhere = pl.BlockSpec(memory_space=pl.ANY)
    vmem = pl.BlockSpec(memory_space=pltpu.VMEM)
    return pl.pallas_call(
        attention_kernel,
        out_shape=[
            jax.ShapeDtypeStruct((rows, HD), jnp.bfloat16),
            jax.ShapeDtypeStruct((rows // HD, HD), jnp.float32),
        ],
        in_specs=[pl.BlockSpec(memory_space=pltpu.SMEM), vmem] + [anywhere] * 4,
        out_specs=[vmem, vmem],
        scratch_shapes=[
            pltpu.VMEM((SLOTS * BLK, HD), jnp.bfloat16),
            pltpu.VMEM((SLOTS * BLK, HD), jnp.bfloat16),
            pltpu.VMEM((TQ, HD), jnp.float32),
            pltpu.VMEM((TQ, HD), jnp.float32),
            pltpu.VMEM((TQ, HD), jnp.float32),
            pltpu.VMEM((TQ, 2 * HD), jnp.float32),
            pltpu.VMEM((TQ, HD), jnp.float32),
            pltpu.SMEM((1,), jnp.int32),
            pltpu.SemaphoreType.DMA((2, SLOTS)),
        ],
        compiler_params=pltpu.CompilerParams(vmem_limit_bytes=56 * MIB),
        cost_estimate=pl.CostEstimate(
            flops=2 * 2 * rows * 2 * BLK * 2 * HD, bytes_accessed=20 * MIB, transcendentals=0
        ),
        name="attention",
    )(choice, q_all, k_own, k_oth, v_own, v_oth)


def merge_kernel(o_ref, lse_ref, out_ref, o_in, lse_in, send, recv):
    ctx = lax.axis_index("ctx")
    exp = lax.axis_index("exp")
    chip = ctx // 2
    core = lax.rem(ctx, 2)
    barrier = pltpu.get_barrier_semaphore()
    for d in range(1, CHIPS):
        peer = 2 * lax.rem(chip + d, CHIPS) + core
        pl.semaphore_signal(barrier, inc=1, device_id=(peer, exp), device_id_type=MESH)
    pl.semaphore_wait(barrier, CHIPS - 1)
    copies = []
    for d in (2, 1, 3):
        to = lax.rem(chip + d, CHIPS)
        peer = (2 * to + core, exp)
        for kind, src, dst in ((0, o_ref, o_in), (1, lse_ref, lse_in)):
            copy = pltpu.make_async_remote_copy(
                src_ref=src.at[to],
                dst_ref=dst.at[d - 1],
                send_sem=send.at[kind, d - 1],
                recv_sem=recv.at[kind, d - 1],
                device_id=peer,
                device_id_type=MESH,
            )
            copy.start()
            copies.append(copy)
    for copy in copies:
        copy.wait()
    parts = [lse_ref[chip]] + [lse_in[d] for d in range(CHIPS - 1)]
    top = functools.reduce(jnp.maximum, parts)
    weights = [jnp.exp2(part - top) for part in parts]
    total = functools.reduce(jnp.add, weights)
    columns = [jnp.transpose(weight / total) for weight in weights]
    for g in range(CHUNK // HD):
        rows = pl.ds(g * HD, HD)
        mixed = columns[0][:, g : g + 1] * o_ref[chip, rows, :].astype(jnp.float32)
        for d in range(CHIPS - 1):
            mixed += columns[d + 1][:, g : g + 1] * o_in[d, rows, :].astype(jnp.float32)
        out_ref[rows, :] = mixed.astype(jnp.bfloat16)


def merge(o, lse):
    vmem = pl.BlockSpec(memory_space=pltpu.VMEM)
    return pl.pallas_call(
        merge_kernel,
        out_shape=jax.ShapeDtypeStruct((CHUNK, HD), jnp.bfloat16),
        in_specs=[vmem, vmem],
        out_specs=vmem,
        scratch_shapes=[
            pltpu.VMEM((CHIPS - 1, CHUNK, HD), jnp.bfloat16),
            pltpu.VMEM((CHIPS - 1, CHUNK // HD, HD), jnp.float32),
            pltpu.SemaphoreType.DMA((2, CHIPS - 1)),
            pltpu.SemaphoreType.DMA((2, CHIPS - 1)),
        ],
        compiler_params=pltpu.CompilerParams(
            collective_id=0, has_side_effects=True, vmem_limit_bytes=32 * MIB
        ),
        name="merge",
    )(o.reshape(CHIPS, CHUNK, HD), lse.reshape(CHIPS, CHUNK // HD, HD))


ROWS = EXPERTS * CAP
FULL = ROWS + TOK


def expert_kernel(
    att_hbm, hid_hbm, proj_hbm, gate_hbm, up_hbm, down_hbm, ids_ref, gain_ref, router_ref,
    y_ref, res_ref,
    att, hid, proj, gate, up, down, picked, wide, normed, inner, sems,
):
    me = lax.axis_index("exp")
    width = hid.shape[1]
    copies = [
        pltpu.make_async_copy(src, dst, sems.at[i])
        for i, (src, dst) in enumerate(
            ((att_hbm, att), (hid_hbm, hid), (proj_hbm, proj), (gate_hbm, gate), (up_hbm, up), (down_hbm, down))
        )
    ]
    for copy in copies:
        copy.start()
    ids = ids_ref[...]
    chosen = functools.reduce(jnp.logical_or, [ids[j : j + 1] == me for j in range(6)])
    chosen_f = jnp.where(chosen, 1.0, 0.0)
    t_from = lax.broadcasted_iota(jnp.int32, (GROUP, GROUP), 0)
    t_to = lax.broadcasted_iota(jnp.int32, (GROUP, GROUP), 1)
    before = jnp.where((t_from < t_to) & (t_from // TOK == t_to // TOK), 1.0, 0.0)
    rank = mm(
        jnp.broadcast_to(chosen_f, (8, GROUP)).astype(jnp.bfloat16), before.astype(jnp.bfloat16)
    )[:1]
    token = lax.broadcasted_iota(jnp.int32, (1, GROUP), 1)
    place = jnp.where(chosen, (token // TOK) * CAP + rank.astype(jnp.int32), -1)
    own_place = jnp.where(token // TOK == me, ROWS + lax.rem(token, TOK), -1)
    row = lax.broadcasted_iota(jnp.int32, (FULL, GROUP), 0)
    select = jnp.where((row == place) | (row == own_place), 1.0, 0.0).astype(jnp.bfloat16)
    expert = lax.broadcasted_iota(jnp.int32, (EXPERTS, GROUP), 0)
    member = functools.reduce(jnp.logical_or, [ids[j : j + 1] == expert for j in range(6)])
    member_rows = nt(select, jnp.where(member, 1.0, 0.0).astype(jnp.bfloat16))
    copies[0].wait()
    for h in range(0, EXPERTS, 2):
        pair = jnp.concatenate([att[h], att[h + 1]], axis=1)
        picked[:, h * HD : (h + 2) * HD] = mm(select, pair).astype(jnp.bfloat16)
    copies[1].wait()
    copies[2].wait()

    step = 2 * HD

    @pl.loop(0, width // step)
    def _(c):
        cols = pl.ds(pl.multiple_of(c * step, step), step)
        base = mm(select, hid[:, cols])
        wide[:, cols] = (base + mm(picked[...], proj[:, cols])).astype(jnp.bfloat16)

    res_ref[...] = wide[ROWS:, :]
    for i in range(0, ROWS, 64):
        part = wide[i : i + 64, :].astype(jnp.float32)
        square = jnp.mean(part * part, axis=1, keepdims=True)
        normed[i : i + 64, :] = (part * lax.rsqrt(square + NORM_EPS) * gain_ref[...]).astype(jnp.bfloat16)
    affinity = jax.nn.sigmoid(mm(normed[...], router_ref[...]))
    lane = lax.broadcasted_iota(jnp.int32, affinity.shape, 1)
    mine = jnp.sum(jnp.where(lane == me, affinity, 0.0), axis=1, keepdims=True)
    everyone = jnp.sum(member_rows[:ROWS] * affinity, axis=1, keepdims=True)
    used = everyone > 0.0
    mix = jnp.where(used, ROUTE_SCALE * mine / jnp.where(used, everyone, 1.0), 0.0)
    copies[3].wait()
    copies[4].wait()
    hidden_units = gate.shape[1]
    for start in range(0, hidden_units, step):
        cols = slice(start, min(start + step, hidden_units))
        g = mm(normed[...], gate[:, cols])
        u = mm(normed[...], up[:, cols])
        inner[:, cols] = (g / (1.0 + jnp.exp(-g)) * u).astype(jnp.bfloat16)
    copies[5].wait()

    @pl.loop(0, width // step)
    def _(c):
        cols = pl.ds(pl.multiple_of(c * step, step), step)
        y_ref[:, cols] = (mm(inner[...], down[:, cols]) * mix).astype(jnp.bfloat16)


def experts(att_all, hid_all, proj_all, w_gate, w_up, w_down, ids_all, gain, router):
    width = hid_all.shape[1]
    units = w_gate.shape[1]
    anywhere = pl.BlockSpec(memory_space=pl.ANY)
    vmem = pl.BlockSpec(memory_space=pltpu.VMEM)
    bf16 = jnp.bfloat16
    return pl.pallas_call(
        expert_kernel,
        out_shape=[
            jax.ShapeDtypeStruct((ROWS, width), bf16),
            jax.ShapeDtypeStruct((TOK, width), bf16),
        ],
        in_specs=[anywhere] * 6 + [vmem] * 3,
        out_specs=[vmem, vmem],
        scratch_shapes=[
            pltpu.VMEM((EXPERTS, GROUP, HD), bf16),
            pltpu.VMEM((GROUP, width), bf16),
            pltpu.VMEM((width, width), bf16),
            pltpu.VMEM((width, units), bf16),
            pltpu.VMEM((width, units), bf16),
            pltpu.VMEM((units, width), bf16),
            pltpu.VMEM((FULL, width), bf16),
            pltpu.VMEM((FULL, width), bf16),
            pltpu.VMEM((ROWS, width), bf16),
            pltpu.VMEM((ROWS, units), bf16),
            pltpu.SemaphoreType.DMA((6,)),
        ],
        compiler_params=pltpu.CompilerParams(vmem_limit_bytes=60 * MIB),
        cost_estimate=pl.CostEstimate(
            flops=20 * 10**9, bytes_accessed=40 * MIB, transcendentals=0
        ),
        name="experts",
    )(att_all, hid_all, proj_all, w_gate, w_up, w_down, ids_all, gain, router)


def local(
    hidden_in, queries, keys, values, block_choice, out_proj, norm_gain, router, expert_ids,
    w_gate, w_up, w_down,
):
    width = hidden_in.shape[1]
    same_core = [[0, 2, 4, 6], [1, 3, 5, 7]]
    swap = [(i, i ^ 1) for i in range(8)]
    k_oth = lax.ppermute(keys, "ctx", swap)
    v_oth = lax.ppermute(values, "ctx", swap)
    q_all = lax.all_gather(queries, "ctx", axis=0, tiled=True, axis_index_groups=same_core)
    proj_all = lax.all_gather(out_proj, "exp", axis=0, tiled=True)
    hid_all = lax.all_gather(hidden_in, "exp", axis=0, tiled=True)
    ids_group = lax.all_gather(expert_ids, "exp", axis=0, tiled=True)
    ids_all = jnp.pad(ids_group.T, ((0, 2), (0, 0)), constant_values=-1)

    o, lse = attend(block_choice, q_all, keys, k_oth, values, v_oth)
    att = merge(o, lse)
    att_all = lax.all_gather(att, "exp", axis=0)
    y, residual = experts(
        att_all, hid_all, proj_all, w_gate[0], w_up[0], w_down[0], ids_all,
        norm_gain.reshape(1, width), router,
    )
    returned = lax.all_to_all(
        y.reshape(EXPERTS, CAP, width), "exp", split_axis=0, concat_axis=0, tiled=True
    ).reshape(ROWS, width)
    hot = expert_ids[:, :, None] == jnp.arange(EXPERTS, dtype=jnp.int32)[None, None, :]
    hot = jnp.any(hot, axis=1)
    rank = jnp.cumsum(hot.astype(jnp.int32), axis=0) - 1
    place = jnp.where(hot, jnp.arange(EXPERTS, dtype=jnp.int32)[None, :] * CAP + rank, -1)
    slot = jnp.arange(ROWS, dtype=jnp.int32)
    gather = jnp.repeat(place, CAP, axis=1, total_repeat_length=ROWS) == slot[None, :]
    combined = mm(gather.astype(jnp.bfloat16), returned)
    return (residual.astype(jnp.float32) + combined).astype(jnp.bfloat16)


def solution(mesh):
    placed = (
        P(("ctx", "exp"), None),
        P("ctx", "exp"),
        P("ctx", "exp"),
        P("ctx", "exp"),
        P(),
        P("exp", None),
        P(),
        P(),
        P(("ctx", "exp"), None),
        P("exp", None, None),
        P("exp", None, None),
        P("exp", None, None),
    )
    return jax.shard_map(
        local, mesh=mesh, in_specs=placed, out_specs=P(("ctx", "exp"), None), check_vma=False
    )
```

```python
import functools

import jax
import jax.numpy as jnp
from jax import lax
from jax.experimental import pallas as pl
from jax.experimental.pallas import tpu as pltpu
from jax.sharding import PartitionSpec as P

HD = 128
BLK = 4096
ROUTE_SCALE = 2.446
NORM_EPS = 1e-06
LOG2E = 1.4426950408889634
LOW = -1e30
JUMP = 100.0
MESH = pl.DeviceIdType.MESH
MIB = 2**20

CHUNK = 1024
TQ = 512
SUB = 128
TKS = 1024
CHIPS = 4
SLOTS = 4
CAP = 36
TOK = 64
EXPERTS = 16
GROUP = EXPERTS * TOK


def nt(a, b):
    return lax.dot_general(a, b, (((1,), (1,)), ((), ())), preferred_element_type=jnp.float32)


def mm(a, b):
    return jnp.dot(a, b, preferred_element_type=jnp.float32)


def attention_kernel(
    choice, q_ref, k_own, k_oth, v_own, v_oth, o_ref, lse_ref,
    k_all, v_all, acc, m_s, l_s, r_s, mx_s, fresh, sems,
):
    scale = HD**-0.5 * LOG2E
    ctx = lax.axis_index("ctx")
    core = lax.rem(ctx, 2)
    other = ctx + 1 - 2 * core
    copies = []
    for slot in range(SLOTS):
        src_k, src_v = (k_own, v_own) if slot < 2 else (k_oth, v_oth)
        src = pl.ds((slot % 2) * BLK, BLK)
        dst = pl.ds(slot * BLK, BLK)
        copies.append(
            (
                pltpu.make_async_copy(src_k.at[src], k_all.at[dst], sems.at[0, slot]),
                pltpu.make_async_copy(src_v.at[src], v_all.at[dst], sems.at[1, slot]),
            )
        )
    for pair in copies:
        for copy in pair:
            copy.start()
    for pair in copies:
        for copy in pair:
            copy.wait()
    ones = jnp.ones((BLK, HD), jnp.bfloat16)

    def careful(q0, slot, steps, reach):
        @pl.loop(0, steps)
        def _(step):
            at = pl.ds(pl.multiple_of(slot * BLK + step * TKS, TKS), TKS)
            keys = k_all[at, :]
            vals = v_all[at, :]
            for i in range(TQ // SUB):
                rows = pl.ds(i * SUB, SUB)
                q = q_ref[pl.ds(pl.multiple_of(q0 + i * SUB, SUB), SUB), :]
                s = nt(q, keys) * scale
                key_pos = step * TKS + lax.broadcasted_iota(jnp.int32, (SUB, TKS), 1)
                query_pos = reach + i * SUB + lax.broadcasted_iota(jnp.int32, (SUB, TKS), 0)
                s = jnp.where(key_pos <= query_pos, s, LOW)
                old = m_s[rows]
                new = jnp.maximum(old, jnp.max(s, axis=1, keepdims=True))
                fade = jnp.exp2(old - new)
                p = jnp.exp2(s - new[:, :1])
                m_s[rows] = new
                l_s[rows] = l_s[rows] * fade + jnp.sum(p, axis=1, keepdims=True)
                acc[rows] = acc[rows] * fade + mm(p.astype(jnp.bfloat16), vals)

    def quick(q0, slot):
        base = pl.multiple_of(slot * BLK, BLK)
        keys = k_all[pl.ds(base, BLK), :]
        vals = jnp.concatenate([v_all[pl.ds(base, BLK), :], ones], axis=1)

        @pl.when(fresh[0] == 1)
        def _():
            some = k_all[pl.ds(base, 256), :]
            s = nt(q_ref[pl.ds(q0, TQ), :], some) * scale
            m_s[...] = jnp.broadcast_to(jnp.max(s, axis=1, keepdims=True), m_s.shape)

        for i in range(TQ // SUB):
            rows = pl.ds(i * SUB, SUB)
            q = q_ref[pl.ds(pl.multiple_of(q0 + i * SUB, SUB), SUB), :]
            s = nt(q, keys)
            old = m_s[rows]
            mx_s[rows] = jnp.broadcast_to(jnp.max(s, axis=1, keepdims=True) * scale, old.shape)
            p = jnp.exp2(s * scale - old[:, :1])
            r_s[rows] = mm(p.astype(jnp.bfloat16), vals)
        jump = jnp.max(mx_s[...] - m_s[...])

        @pl.when(jump <= JUMP)
        def _():
            old = m_s[...]
            new = jnp.maximum(old, mx_s[...])
            fade = jnp.exp2(old - new)
            m_s[...] = new
            acc[...] = (acc[...] + r_s[:, :HD]) * fade
            l_s[...] = (l_s[...] + r_s[:, HD:]) * fade

        @pl.when(jnp.logical_not(jump <= JUMP))
        def _():
            careful(q0, slot, BLK // TKS, BLK)

    @pl.loop(0, CHIPS * CHUNK // TQ)
    def _(tile):
        q0 = pl.multiple_of(tile * TQ, TQ)
        chunk = tile // (CHUNK // TQ)
        row = 14 + chunk // 2
        in_block = lax.rem(2 * chunk + core, 4) * CHUNK + lax.rem(tile, CHUNK // TQ) * TQ
        acc[...] = jnp.zeros_like(acc)
        l_s[...] = jnp.zeros_like(l_s)
        m_s[...] = jnp.full_like(m_s, LOW)
        fresh[0] = 1

        @pl.loop(0, SLOTS)
        def _(slot):
            block = jnp.where(slot < 2, 2 * ctx + slot, 2 * other + slot - 2)
            hit = choice[row, 1] == block
            for j in range(2, 8):
                hit = jnp.logical_or(hit, choice[row, j] == block)
            own = block == row

            @pl.when(own)
            def _():
                careful(q0, slot, in_block // TKS + 1, in_block)
                fresh[0] = 0

            @pl.when(jnp.logical_and(hit, jnp.logical_not(own)))
            def _():
                quick(q0, slot)
                fresh[0] = 0

        total = l_s[...]
        some = total > 0.0
        total = jnp.where(some, total, 1.0)
        o_ref[pl.ds(q0, TQ), :] = (acc[...] / total).astype(jnp.bfloat16)
        lse = jnp.where(some, m_s[...] + jnp.log2(total), LOW)
        flat = jnp.transpose(lse)
        for i in range(TQ // HD):
            lse_ref[pl.ds(tile * (TQ // HD) + i, 1), :] = flat[:1, i * HD : (i + 1) * HD]


def attend(choice, q_all, k_own, k_oth, v_own, v_oth):
    rows = CHIPS * CHUNK
    anywhere = pl.BlockSpec(memory_space=pl.ANY)
    vmem = pl.BlockSpec(memory_space=pltpu.VMEM)
    return pl.pallas_call(
        attention_kernel,
        out_shape=[
            jax.ShapeDtypeStruct((rows, HD), jnp.bfloat16),
            jax.ShapeDtypeStruct((rows // HD, HD), jnp.float32),
        ],
        in_specs=[pl.BlockSpec(memory_space=pltpu.SMEM), vmem] + [anywhere] * 4,
        out_specs=[vmem, vmem],
        scratch_shapes=[
            pltpu.VMEM((SLOTS * BLK, HD), jnp.bfloat16),
            pltpu.VMEM((SLOTS * BLK, HD), jnp.bfloat16),
            pltpu.VMEM((TQ, HD), jnp.float32),
            pltpu.VMEM((TQ, HD), jnp.float32),
            pltpu.VMEM((TQ, HD), jnp.float32),
            pltpu.VMEM((TQ, 2 * HD), jnp.float32),
            pltpu.VMEM((TQ, HD), jnp.float32),
            pltpu.SMEM((1,), jnp.int32),
            pltpu.SemaphoreType.DMA((2, SLOTS)),
        ],
        compiler_params=pltpu.CompilerParams(vmem_limit_bytes=56 * MIB),
        cost_estimate=pl.CostEstimate(
            flops=2 * 2 * rows * 2 * BLK * 2 * HD, bytes_accessed=20 * MIB, transcendentals=0
        ),
        name="attention",
    )(choice, q_all, k_own, k_oth, v_own, v_oth)


def share_kernel(q_ref, k_ref, v_ref, ids_ref, q_all, k_oth, v_oth, ids_all, send, recv, near):
    ctx = lax.axis_index("ctx")
    me = lax.axis_index("exp")
    chip = ctx // 2
    core = lax.rem(ctx, 2)
    twin = (ctx + 1 - 2 * core, me)
    x_peers = [(2 * lax.rem(chip + d, CHIPS) + core, me) for d in range(1, CHIPS)]
    e_peers = [(ctx, lax.rem(me + d, EXPERTS)) for d in range(1, EXPERTS)]
    barrier = pltpu.get_barrier_semaphore()
    for peer in [twin] + x_peers + e_peers:
        pl.semaphore_signal(barrier, inc=1, device_id=peer, device_id_type=MESH)
    mine = [
        pltpu.make_async_copy(q_ref, q_all.at[chip], near.at[0]),
        pltpu.make_async_copy(ids_ref, ids_all.at[me], near.at[1]),
    ]
    for copy in mine:
        copy.start()
    pl.semaphore_wait(barrier, 1 + len(x_peers) + len(e_peers))
    copies = []

    def send_to(src, dst, peer):
        n = len(copies)
        copy = pltpu.make_async_remote_copy(
            src_ref=src, dst_ref=dst, send_sem=send.at[n], recv_sem=recv.at[n],
            device_id=peer, device_id_type=MESH,
        )
        copy.start()
        copies.append(copy)

    for d in (2, 1, 3):
        send_to(q_ref, q_all.at[chip], x_peers[d - 1])
    for part in range(2):
        at = pl.ds(part * BLK, BLK)
        send_to(k_ref.at[at], k_oth.at[at], twin)
        send_to(v_ref.at[at], v_oth.at[at], twin)
    for peer in e_peers:
        send_to(ids_ref, ids_all.at[me], peer)
    for copy in copies + mine:
        copy.wait()


def share(queries, keys, values, ids):
    anywhere = pl.BlockSpec(memory_space=pl.ANY)
    copies = CHIPS - 1 + 4 + EXPERTS - 1
    return pl.pallas_call(
        share_kernel,
        out_shape=[
            jax.ShapeDtypeStruct((CHIPS,) + queries.shape, queries.dtype),
            jax.ShapeDtypeStruct(keys.shape, keys.dtype),
            jax.ShapeDtypeStruct(values.shape, values.dtype),
            jax.ShapeDtypeStruct((EXPERTS,) + ids.shape, ids.dtype),
        ],
        in_specs=[anywhere] * 4,
        out_specs=[anywhere] * 4,
        scratch_shapes=[
            pltpu.SemaphoreType.DMA((copies,)),
            pltpu.SemaphoreType.DMA((copies,)),
            pltpu.SemaphoreType.DMA((2,)),
        ],
        compiler_params=pltpu.CompilerParams(collective_id=0, has_side_effects=True),
        name="share",
    )(queries, keys, values, ids)


SIDE = 4
PACK = SIDE * CAP
LINE = SIDE * TOK
ROWS = EXPERTS * CAP
HALF = 1024
STEP = 256


def post_kernel(
    o_ref, lse_ref, hid_ref, ids_ref, gain_ref, router_ref, proj_hbm, gate_hbm, up_hbm, down_hbm,
    out_ref,
    o_in, lse_in, att, heads, proj, gate, up, down, wide, nall, picked, inner, turned, y_out,
    y_in, z_out, z_in,
    near, x_send, x_recv, a_send, a_recv, g_send, g_recv, r_send, r_recv,
):
    ctx = lax.axis_index("ctx")
    me = lax.axis_index("exp")
    chip = ctx // 2
    core = lax.rem(ctx, 2)
    yy = me // SIDE
    zz = lax.rem(me, SIDE)
    width = hid_ref.shape[1]

    def along(axis, d):
        if axis == 0:
            return lax.rem(yy + d, SIDE) * SIDE + zz
        return yy * SIDE + lax.rem(zz + d, SIDE)

    loads = [
        pltpu.make_async_copy(src, dst, near.at[i])
        for i, (src, dst) in enumerate(
            ((proj_hbm, proj), (gate_hbm, gate), (up_hbm, up), (down_hbm, down))
        )
    ]
    for load in loads:
        load.start()
    barrier = pltpu.get_barrier_semaphore()
    for d in range(1, CHIPS):
        peer = (2 * lax.rem(chip + d, CHIPS) + core, me)
        pl.semaphore_signal(barrier, inc=1, device_id=peer, device_id_type=MESH)
    for d in range(1, EXPERTS):
        peer = (ctx, lax.rem(me + d, EXPERTS))
        pl.semaphore_signal(barrier, inc=1, device_id=peer, device_id_type=MESH)
    pl.semaphore_wait(barrier, CHIPS - 1 + EXPERTS - 1)

    def remote(src, dst, send, recv, peer):
        copy = pltpu.make_async_remote_copy(
            src_ref=src, dst_ref=dst, send_sem=send, recv_sem=recv,
            device_id=peer, device_id_type=MESH,
        )
        copy.start()
        return copy

    x_copies = []
    for d in (2, 1, 3):
        to = lax.rem(chip + d, CHIPS)
        peer = (2 * to + core, me)
        for kind, src, dst in ((0, o_ref, o_in), (1, lse_ref, lse_in)):
            x_copies.append(
                remote(src.at[to], dst.at[d - 1], x_send.at[kind, d - 1], x_recv.at[kind, d - 1], peer)
            )

    t_to = lax.broadcasted_iota(jnp.int32, (LINE, LINE), 0)
    t_from = lax.broadcasted_iota(jnp.int32, (LINE, LINE), 1)
    before = jnp.where((t_from < t_to) & (t_from // TOK == t_to // TOK), 1.0, 0.0).astype(jnp.bfloat16)
    base = (lax.broadcasted_iota(jnp.int32, (LINE, HD), 0) // TOK) * CAP
    slot = lax.broadcasted_iota(jnp.int32, (LINE, LINE), 1)

    def packing(ids, expert):
        chosen = functools.reduce(jnp.logical_or, [ids[:, j : j + 1] == expert for j in range(6)])
        chosen = jnp.broadcast_to(chosen, (LINE, HD))
        rank = mm(before, jnp.where(chosen, 1.0, 0.0).astype(jnp.bfloat16)).astype(jnp.int32)
        place = jnp.where(chosen, base + rank, -1)
        return jnp.where(slot == place[:, :1], 1.0, 0.0)

    lane = lax.broadcasted_iota(jnp.int32, (LINE, HD), 1)
    selects = []
    members = []
    for g in range(SIDE):
        ids = jnp.concatenate([ids_ref[g * SIDE + i] for i in range(SIDE)], axis=0)
        select = jnp.transpose(packing(ids, me))[:PACK].astype(jnp.bfloat16)
        member = functools.reduce(jnp.logical_or, [ids[:, j : j + 1] == lane for j in range(6)])
        selects.append(select)
        members.append(mm(select, jnp.where(member, 1.0, 0.0).astype(jnp.bfloat16)))

    for copy in x_copies:
        copy.wait()
    parts = [lse_ref[chip]] + [lse_in[d] for d in range(CHIPS - 1)]
    top = functools.reduce(jnp.maximum, parts)
    weights = [jnp.exp2(part - top) for part in parts]
    total = functools.reduce(jnp.add, weights)
    columns = [jnp.transpose(weight / total) for weight in weights]
    for g in range(CHUNK // HD):
        rows = pl.ds(g * HD, HD)
        mixed = columns[0][:, g : g + 1] * o_ref[chip, rows, :].astype(jnp.float32)
        for d in range(CHIPS - 1):
            mixed += columns[d + 1][:, g : g + 1] * o_in[d, rows, :].astype(jnp.float32)
        att[2 * g] = mixed[:TOK].astype(jnp.bfloat16)
        att[2 * g + 1] = mixed[TOK:].astype(jnp.bfloat16)
    a_copies = []
    for d in range(1, EXPERTS):
        to = lax.rem(me + d, EXPERTS)
        a_copies.append(
            remote(att.at[to], heads.at[me], a_send.at[d - 1], a_recv.at[d - 1], (ctx, to))
        )
    heads[me] = att[me]
    loads[0].wait()
    for copy in a_copies:
        copy.wait()
    joined = jnp.concatenate([heads[h] for h in range(EXPERTS)], axis=1)

    @pl.loop(0, width // STEP)
    def _(c):
        cols = pl.ds(pl.multiple_of(c * STEP, STEP), STEP)
        wide[:, cols] = hid_ref[:, cols].astype(jnp.float32) + mm(joined, proj[:, cols])

    residual = wide[...].astype(jnp.bfloat16).astype(jnp.float32)
    wide[...] = residual
    square = jnp.mean(residual * residual, axis=1, keepdims=True)
    normed = (residual * lax.rsqrt(square + NORM_EPS) * gain_ref[...]).astype(jnp.bfloat16)
    nall[0, me] = normed[:, :HALF]
    nall[1, me] = normed[:, HALF:]

    top_rows, low_rows = pl.ds(0, TOK // 2), pl.ds(TOK // 2, TOK // 2)
    g_copies = []

    def pass_on(half, owner, rows, axis, d, n):
        view = nall.at[half, owner] if rows is None else nall.at[half, owner, rows]
        copy = remote(view, view, g_send.at[half, n], g_recv.at[half, n], (ctx, along(axis, d)))
        g_copies.append(copy)
        return copy

    def owner_at(half, first, second):
        dy, dz = (second, first) if half == 0 else (first, second)
        return lax.rem(yy + dy, SIDE) * SIDE + lax.rem(zz + dz, SIDE)

    firsts = (1, 0)
    seconds = (0, 1)
    stage1 = {}
    stage2 = {}
    for half in range(2):
        for n, d in ((0, 1), (1, 3)):
            stage1[half, d] = pass_on(half, me, None, firsts[half], d, n)
        for n, d in ((4, 1), (5, 3)):
            stage2[half, 0, d] = pass_on(half, me, None, seconds[half], d, n)
    for half in range(2):
        stage1[half, 1].wait_recv()
        stage1[half, 10] = pass_on(half, owner_at(half, 3, 0), top_rows, firsts[half], 1, 2)
        stage1[half, 3].wait_recv()
        stage1[half, 30] = pass_on(half, owner_at(half, 1, 0), low_rows, firsts[half], 3, 3)
        for first, n in ((3, 8), (1, 12)):
            for d in (1, 3):
                stage2[half, first, d] = pass_on(
                    half, owner_at(half, first, 0), None, seconds[half], d, n + d // 2
                )
    for half in range(2):
        stage2[half, 0, 1].wait_recv()
        pass_on(half, owner_at(half, 0, 3), top_rows, seconds[half], 1, 6)
        stage2[half, 0, 3].wait_recv()
        pass_on(half, owner_at(half, 0, 1), low_rows, seconds[half], 3, 7)
    for half in range(2):
        stage1[half, 10].wait_recv()
        stage1[half, 30].wait_recv()
        for d in (1, 3):
            stage2[half, 2, d] = pass_on(
                half, owner_at(half, 2, 0), None, seconds[half], d, 16 + d // 2
            )
    for first, n in ((3, 10), (1, 14), (2, 18)):
        for half in range(2):
            stage2[half, first, 1].wait_recv()
            pass_on(half, owner_at(half, first, 3), top_rows, seconds[half], 1, n)
            stage2[half, first, 3].wait_recv()
            pass_on(half, owner_at(half, first, 1), low_rows, seconds[half], 3, n + 1)
    arrived = list(stage1.values()) + list(stage2.values())
    for copy in g_copies:
        if not any(copy is seen for seen in arrived):
            copy.wait_recv()
    for copy in g_copies:
        copy.wait_send()

    for g in range(SIDE):
        rows = pl.ds(g * PACK, PACK)
        for half in range(2):
            line = jnp.concatenate([nall[half, g * SIDE + i] for i in range(SIDE)], axis=0)
            picked[rows, half * HALF : (half + 1) * HALF] = mm(selects[g], line).astype(jnp.bfloat16)
    affinity = jax.nn.sigmoid(mm(picked[...], router_ref[...]))
    expert = lax.broadcasted_iota(jnp.int32, affinity.shape, 1)
    mine = jnp.sum(jnp.where(expert == me, affinity, 0.0), axis=1, keepdims=True)
    member = jnp.concatenate(members, axis=0)
    everyone = jnp.sum(member[:, :EXPERTS] * affinity, axis=1, keepdims=True)
    used = everyone > 0.0
    mix = jnp.where(used, ROUTE_SCALE * mine / jnp.where(used, everyone, 1.0), 0.0)
    loads[1].wait()
    loads[2].wait()
    units = gate.shape[1]
    for start in range(0, units, STEP):
        cols = slice(start, min(start + STEP, units))
        gated = mm(picked[...], gate[:, cols])
        raised = mm(picked[...], up[:, cols])
        inner[:, cols] = (gated / (1.0 + jnp.exp(-gated)) * raised).astype(jnp.bfloat16)
    to_row = lax.broadcasted_iota(jnp.int32, (ROWS, ROWS), 0)
    from_row = lax.broadcasted_iota(jnp.int32, (ROWS, ROWS), 1)
    owner = to_row // CAP
    source = (lax.rem(owner, SIDE) * SIDE + owner // SIDE) * CAP + lax.rem(to_row, CAP)
    turn = jnp.where(from_row == source, 1.0, 0.0).astype(jnp.bfloat16)
    turned[...] = mm(turn, inner[...]).astype(jnp.bfloat16)
    mix_high = mix.astype(jnp.bfloat16)
    mix_low = (mix - mix_high.astype(jnp.float32)).astype(jnp.bfloat16)
    mix_turned = mm(turn, jnp.broadcast_to(mix_high, (ROWS, HD))) + mm(
        turn, jnp.broadcast_to(mix_low, (ROWS, HD))
    )
    loads[3].wait()
    r_copies = {}
    for half in range(2):
        rows_in = inner if half == 0 else turned
        share_of = mix if half == 0 else mix_turned[:, :1]

        @pl.loop(0, HALF // STEP)
        def _(c):
            cols = pl.ds(pl.multiple_of(c * STEP, STEP), STEP)
            from_cols = pl.ds(pl.multiple_of(half * HALF + c * STEP, STEP), STEP)
            y = mm(rows_in[...], down[:, from_cols]) * share_of
            for g in range(SIDE):
                y_out[half, g, :, cols] = y[g * PACK : (g + 1) * PACK].astype(jnp.bfloat16)

        at = yy if half == 0 else zz
        for d in (2, 1, 3):
            r_copies[half, 0, d] = remote(
                y_out.at[half, lax.rem(at + d, SIDE)], y_in.at[half, d - 1],
                r_send.at[half, 0, d - 1], r_recv.at[half, 0, d - 1], (ctx, along(half, d)),
            )

    sums = []
    for half in range(2):
        at = yy if half == 0 else zz
        owners = [yy * SIDE + i if half == 0 else i * SIDE + zz for i in range(SIDE)]
        ids = jnp.concatenate([ids_ref[owner] for owner in owners], axis=0)
        summed = mm(
            packing(ids, me)[:, :PACK].astype(jnp.bfloat16), y_out[half, at]
        )
        for d in (1, 3, 2):
            expert_from = along(half, SIDE - d)
            spread = packing(ids, expert_from)[:, :PACK].astype(jnp.bfloat16)
            r_copies[half, 0, d].wait_recv()
            summed += mm(spread, y_in[half, d - 1])
        for i in range(SIDE):
            z_out[half, i] = summed[i * TOK : (i + 1) * TOK].astype(jnp.bfloat16)
        here = zz if half == 0 else yy
        for d in (2, 1, 3):
            r_copies[half, 1, d] = remote(
                z_out.at[half, lax.rem(here + d, SIDE)], z_in.at[half, d - 1],
                r_send.at[half, 1, d - 1], r_recv.at[half, 1, d - 1], (ctx, along(1 - half, d)),
            )
    for half in range(2):
        here = zz if half == 0 else yy
        cols = slice(half * HALF, (half + 1) * HALF)
        result = wide[:, cols] + z_out[half, here].astype(jnp.float32)
        for d in (1, 3, 2):
            r_copies[half, 1, d].wait_recv()
            result += z_in[half, d - 1].astype(jnp.float32)
        out_ref[:, cols] = result.astype(jnp.bfloat16)
    for copy in r_copies.values():
        copy.wait_send()


def post(o, lse, hidden_in, ids, gain, router, proj, w_gate, w_up, w_down):
    width = hidden_in.shape[1]
    units = w_gate.shape[1]
    anywhere = pl.BlockSpec(memory_space=pl.ANY)
    vmem = pl.BlockSpec(memory_space=pltpu.VMEM)
    bf16 = jnp.bfloat16
    dma = pltpu.SemaphoreType.DMA
    return pl.pallas_call(
        post_kernel,
        out_shape=jax.ShapeDtypeStruct((TOK, width), bf16),
        in_specs=[vmem] * 6 + [anywhere] * 4,
        out_specs=vmem,
        scratch_shapes=[
            pltpu.VMEM((CHIPS - 1, CHUNK, HD), bf16),
            pltpu.VMEM((CHIPS - 1, CHUNK // HD, HD), jnp.float32),
            pltpu.VMEM((EXPERTS, TOK, HD), bf16),
            pltpu.VMEM((EXPERTS, TOK, HD), bf16),
            pltpu.VMEM((width, width), bf16),
            pltpu.VMEM((width, units), bf16),
            pltpu.VMEM((width, units), bf16),
            pltpu.VMEM((units, width), bf16),
            pltpu.VMEM((TOK, width), jnp.float32),
            pltpu.VMEM((2, EXPERTS, TOK, HALF), bf16),
            pltpu.VMEM((ROWS, width), bf16),
            pltpu.VMEM((ROWS, units), bf16),
            pltpu.VMEM((ROWS, units), bf16),
            pltpu.VMEM((2, SIDE, PACK, HALF), bf16),
            pltpu.VMEM((2, SIDE - 1, PACK, HALF), bf16),
            pltpu.VMEM((2, SIDE, TOK, HALF), bf16),
            pltpu.VMEM((2, SIDE - 1, TOK, HALF), bf16),
            dma((4,)),
            dma((2, CHIPS - 1)),
            dma((2, CHIPS - 1)),
            dma((EXPERTS - 1,)),
            dma((EXPERTS - 1,)),
            dma((2, 20)),
            dma((2, 20)),
            dma((2, 2, SIDE - 1)),
            dma((2, 2, SIDE - 1)),
        ],
        compiler_params=pltpu.CompilerParams(
            collective_id=1, has_side_effects=True, vmem_limit_bytes=62 * MIB
        ),
        name="post",
    )(
        o.reshape(CHIPS, CHUNK, HD), lse.reshape(CHIPS, CHUNK // HD, HD), hidden_in, ids, gain,
        router, proj, w_gate, w_up, w_down,
    )


def local(
    hidden_in, queries, keys, values, block_choice, out_proj, norm_gain, router, expert_ids,
    w_gate, w_up, w_down,
):
    width = hidden_in.shape[1]
    proj_all = lax.all_gather(out_proj, "exp", axis=0, tiled=True)
    ids = jnp.pad(expert_ids, ((0, 0), (0, HD - expert_ids.shape[1])), constant_values=-1)
    q_all, k_oth, v_oth, ids_all = share(queries, keys, values, ids)
    o, lse = attend(
        block_choice, q_all.reshape(CHIPS * CHUNK, HD), keys, k_oth, values, v_oth
    )
    return post(
        o, lse, hidden_in, ids_all, norm_gain.reshape(1, width), router, proj_all,
        w_gate[0], w_up[0], w_down[0],
    )


def solution(mesh):
    placed = (
        P(("ctx", "exp"), None),
        P("ctx", "exp"),
        P("ctx", "exp"),
        P("ctx", "exp"),
        P(),
        P("exp", None),
        P(),
        P(),
        P(("ctx", "exp"), None),
        P("exp", None, None),
        P("exp", None, None),
        P("exp", None, None),
    )
    return jax.shard_map(
        local, mesh=mesh, in_specs=placed, out_specs=P(("ctx", "exp"), None), check_vma=False
    )
```

```python
import functools

import jax
import jax.numpy as jnp
from jax import lax
from jax.experimental import pallas as pl
from jax.experimental.pallas import tpu as pltpu
from jax.sharding import PartitionSpec as P

HD = 128
BLK = 4096
ROUTE_SCALE = 2.446
NORM_EPS = 1e-06
LOG2E = 1.4426950408889634
LOW = -1e30
JUMP = 100.0
MESH = pl.DeviceIdType.MESH
MIB = 2**20

CHUNK = 1024
TQ = 512
SUB = 128
TKS = 1024
CHIPS = 4
SLOTS = 4
CAP = 36
TOK = 64
EXPERTS = 16
GROUP = EXPERTS * TOK


def nt(a, b):
    return lax.dot_general(a, b, (((1,), (1,)), ((), ())), preferred_element_type=jnp.float32)


def mm(a, b):
    return jnp.dot(a, b, preferred_element_type=jnp.float32)


def attention_kernel(rels, *refs):
    n = len(rels)
    choice, *q_hbm = refs[: 1 + n]
    k_own, k_oth, v_own, v_oth, o_ref, lse_ref = refs[1 + n : 7 + n]
    q_s, k_all, v_all, acc, m_s, l_s, r_s, mx_s, fresh, sems, q_sems = refs[7 + n :]
    scale = HD**-0.5 * LOG2E
    ctx = lax.axis_index("ctx")
    chip = ctx // 2
    core = lax.rem(ctx, 2)
    other = ctx + 1 - 2 * core
    q_copies = [
        pltpu.make_async_copy(q, q_s.at[pl.ds(i * CHUNK, CHUNK)], q_sems.at[i])
        for i, q in enumerate(q_hbm)
    ]
    for copy in q_copies:
        copy.start()
    for slot in range(SLOTS):
        src_k, src_v = (k_own, v_own) if slot < 2 else (k_oth, v_oth)
        src = pl.ds((slot % 2) * BLK, BLK)
        dst = pl.ds(slot * BLK, BLK)
        pltpu.make_async_copy(src_k.at[src], k_all.at[dst], sems.at[0, slot]).start()
        pltpu.make_async_copy(src_v.at[src], v_all.at[dst], sems.at[1, slot]).start()
    for copy in q_copies:
        copy.wait()
    ones = jnp.ones((BLK, HD), jnp.bfloat16)

    def queries(q0, i):
        return q_s[pl.ds(pl.multiple_of(q0 + i * SUB, SUB), SUB), :]

    def masked(s, first_key, first_query):
        key = first_key + lax.broadcasted_iota(jnp.int32, s.shape, 1)
        query = first_query + lax.broadcasted_iota(jnp.int32, s.shape, 0)
        return jnp.where(key <= query, s, LOW)

    def careful(q0, slot, first_key, steps, reach):
        @pl.loop(0, steps)
        def _(step):
            start = first_key + step * TKS
            at = pl.ds(pl.multiple_of(slot * BLK + start, TKS), TKS)
            for i in range(TQ // SUB):
                rows = pl.ds(i * SUB, SUB)
                s = masked(nt(queries(q0, i), k_all[at, :]) * scale, start, reach + i * SUB)
                old = m_s[rows]
                new = jnp.maximum(old, jnp.max(s, axis=1, keepdims=True))
                fade = jnp.exp2(old - new)
                p = jnp.exp2(s - new[:, :1])
                m_s[rows] = new
                l_s[rows] = l_s[rows] * fade + jnp.sum(p, axis=1, keepdims=True)
                acc[rows] = acc[rows] * fade + mm(p.astype(jnp.bfloat16), v_all[at, :])

    def quick(q0, slot, first_key, size, reach, mask):
        base = pl.multiple_of(slot * BLK + first_key, size)
        keys = k_all[pl.ds(base, size), :]
        vals = jnp.concatenate([v_all[pl.ds(base, size), :], ones[:size]], axis=1)
        for i in range(TQ // SUB):
            rows = pl.ds(i * SUB, SUB)
            s = nt(queries(q0, i), keys)
            if mask:
                s = masked(s, first_key, reach + i * SUB)
            old = m_s[rows]
            mx_s[rows] = jnp.broadcast_to(jnp.max(s, axis=1, keepdims=True) * scale, old.shape)
            p = jnp.exp2(s * scale - old[:, :1])
            r_s[rows] = mm(p.astype(jnp.bfloat16), vals)
        jump = jnp.max(mx_s[...] - m_s[...])

        @pl.when(jump <= JUMP)
        def _():
            old = m_s[...]
            new = jnp.maximum(old, mx_s[...])
            fade = jnp.exp2(old - new)
            m_s[...] = new
            acc[...] = (acc[...] + r_s[:, :HD]) * fade
            l_s[...] = (l_s[...] + r_s[:, HD:]) * fade

        @pl.when(jnp.logical_not(jump <= JUMP))
        def _():
            careful(q0, slot, first_key, size // TKS, reach)

    @pl.loop(0, n * CHUNK // TQ)
    def _(tile):
        q0 = pl.multiple_of(tile * TQ, TQ)
        chunk = lax.rem(chip + rels[0] + tile // (CHUNK // TQ), CHIPS)
        row = 14 + chunk // 2
        in_block = lax.rem(2 * chunk + core, 4) * CHUNK + lax.rem(tile, CHUNK // TQ) * TQ
        acc[...] = jnp.zeros_like(acc)
        l_s[...] = jnp.zeros_like(l_s)
        fresh[0] = 1

        @pl.loop(0, SLOTS)
        def _(slot):
            @pl.when(tile == 0)
            def _():
                at = pl.ds(pl.multiple_of(slot * BLK, BLK), BLK)
                first = pl.ds(0, BLK)
                pltpu.make_async_copy(k_own.at[first], k_all.at[at], sems.at[0, slot]).wait()
                pltpu.make_async_copy(v_own.at[first], v_all.at[at], sems.at[1, slot]).wait()

            block = jnp.where(slot < 2, 2 * ctx + slot, 2 * other + slot - 2)
            hit = choice[1, row] == block
            for j in range(2, 8):
                hit = jnp.logical_or(hit, choice[j, row] == block)
            own = block == row
            reach = jnp.where(own, in_block, BLK)

            @pl.when(jnp.logical_and(fresh[0] == 1, jnp.logical_or(own, hit)))
            def _():
                some = k_all[pl.ds(pl.multiple_of(slot * BLK, BLK), 256), :]
                s = masked(nt(q_s[pl.ds(q0, TQ), :], some) * scale, 0, reach)
                m_s[...] = jnp.broadcast_to(jnp.max(s, axis=1, keepdims=True), m_s.shape)
                fresh[0] = 0

            @pl.when(own)
            def _():
                last = in_block // TKS

                @pl.loop(0, last)
                def _(step):
                    quick(q0, slot, pl.multiple_of(step * TKS, TKS), TKS, reach, False)

                quick(q0, slot, pl.multiple_of(last * TKS, TKS), TKS, reach, True)

            @pl.when(jnp.logical_and(hit, jnp.logical_not(own)))
            def _():
                quick(q0, slot, 0, BLK, reach, False)

        total = l_s[...]
        some = total > 0.0
        total = jnp.where(some, total, 1.0)
        o_ref[pl.ds(q0, TQ), :] = (acc[...] / total).astype(jnp.bfloat16)
        lse = jnp.where(some, m_s[...] + jnp.log2(total), LOW)
        flat = jnp.transpose(lse)
        for i in range(TQ // HD):
            lse_ref[pl.ds(tile * (TQ // HD) + i, 1), :] = flat[:1, i * HD : (i + 1) * HD]


def attend(rels, choice, q_parts, k_own, k_oth, v_own, v_oth):
    n = len(rels)
    rows = n * CHUNK
    anywhere = pl.BlockSpec(memory_space=pl.ANY)
    vmem = pl.BlockSpec(memory_space=pltpu.VMEM)
    o, lse = pl.pallas_call(
        functools.partial(attention_kernel, rels),
        out_shape=[
            jax.ShapeDtypeStruct((rows, HD), jnp.bfloat16),
            jax.ShapeDtypeStruct((rows // HD, HD), jnp.float32),
        ],
        in_specs=[pl.BlockSpec(memory_space=pltpu.SMEM)] + [anywhere] * (4 + n),
        out_specs=[vmem, vmem],
        scratch_shapes=[
            pltpu.VMEM((rows, HD), jnp.bfloat16),
            pltpu.VMEM((SLOTS * BLK, HD), jnp.bfloat16),
            pltpu.VMEM((SLOTS * BLK, HD), jnp.bfloat16),
            pltpu.VMEM((TQ, HD), jnp.float32),
            pltpu.VMEM((TQ, HD), jnp.float32),
            pltpu.VMEM((TQ, HD), jnp.float32),
            pltpu.VMEM((TQ, 2 * HD), jnp.float32),
            pltpu.VMEM((TQ, HD), jnp.float32),
            pltpu.SMEM((1,), jnp.int32),
            pltpu.SemaphoreType.DMA((2, SLOTS)),
            pltpu.SemaphoreType.DMA((n,)),
        ],
        compiler_params=pltpu.CompilerParams(vmem_limit_bytes=60 * MIB),
        cost_estimate=pl.CostEstimate(
            flops=2 * 2 * rows * 2 * BLK * 2 * HD, bytes_accessed=10 * MIB, transcendentals=0
        ),
        name="attention_" + "_".join(str(rel) for rel in rels),
    )(choice, *q_parts, k_own, k_oth, v_own, v_oth)
    return o.reshape(n, CHUNK, HD), lse.reshape(n, CHUNK // HD, HD)


SIDE = 4
PACK = SIDE * CAP
LINE = SIDE * TOK
ROWS = EXPERTS * CAP
HALF = 1024
PART = 512
PARTS = HALF // PART
BACK = 512
BACKS = HALF // BACK
STEP = 256


def post_kernel(
    o0_ref, o_ref, lse0_ref, lse_ref, hid_ref, ids_ref, gain_ref, router_ref,
    proj_hbm, gate_hbm, up_hbm, down_hbm,
    out_ref,
    o_in, lse_in, ids_all, att, heads, proj, gate, up, down, wide, packs, place_t, turn,
    line, mixes, pick_out, pick_in, x_turned, sums, inner, turned, y_out, y_in, z_out, z_in,
    near, x_send, x_recv, i_send, i_recv, a_send, a_recv, l_send, l_recv, m_send, m_recv,
    p_send, p_recv, r_send, r_recv,
):
    ctx = lax.axis_index("ctx")
    me = lax.axis_index("exp")
    chip = ctx // 2
    core = lax.rem(ctx, 2)
    yy = me // SIDE
    zz = lax.rem(me, SIDE)
    width = hid_ref.shape[1]
    bf16 = jnp.bfloat16

    def along(axis, d):
        if axis == 0:
            return lax.rem(yy + d, SIDE) * SIDE + zz
        return yy * SIDE + lax.rem(zz + d, SIDE)

    firsts = (1, 0)
    seconds = (0, 1)
    at_first = (zz, yy)
    at_second = (yy, zz)

    loads = [
        pltpu.make_async_copy(src, dst, near.at[i])
        for i, (src, dst) in enumerate(
            ((proj_hbm, proj), (gate_hbm, gate), (up_hbm, up), (down_hbm, down))
        )
    ]
    for load in loads:
        load.start()
    barrier = pltpu.get_barrier_semaphore()
    for d in range(1, CHIPS):
        peer = (2 * lax.rem(chip + d, CHIPS) + core, me)
        pl.semaphore_signal(barrier, inc=1, device_id=peer, device_id_type=MESH)
    for d in range(1, EXPERTS):
        peer = (ctx, lax.rem(me + d, EXPERTS))
        pl.semaphore_signal(barrier, inc=1, device_id=peer, device_id_type=MESH)
    ids_all[me] = jnp.full((TOK, HD), -1, jnp.int32)
    own_ids = jnp.transpose(ids_ref[...].astype(jnp.float32)).astype(jnp.int32)
    ids_all[me, :, :6] = own_ids
    pl.semaphore_wait(barrier, CHIPS - 1 + EXPERTS - 1)

    def remote(src, dst, send, recv, peer):
        copy = pltpu.make_async_remote_copy(
            src_ref=src, dst_ref=dst, send_sem=send, recv_sem=recv,
            device_id=peer, device_id_type=MESH,
        )
        copy.start()
        return copy

    i_copies = []
    for d in range(1, EXPERTS):
        peer = (ctx, lax.rem(me + d, EXPERTS))
        i_copies.append(
            remote(ids_all.at[me], ids_all.at[me], i_send.at[d - 1], i_recv.at[d - 1], peer)
        )
    x_copies = []
    for d in (2, 1, 3):
        peer = (2 * lax.rem(chip + d, CHIPS) + core, me)
        for kind, src, dst in ((0, o_ref, o_in), (1, lse_ref, lse_in)):
            x_copies.append(
                remote(
                    src.at[d - 1], dst.at[d - 1], x_send.at[kind, d - 1], x_recv.at[kind, d - 1],
                    peer,
                )
            )
    to_row = lax.broadcasted_iota(jnp.int32, (ROWS, HD), 0)
    owner = to_row // CAP
    source = (lax.rem(owner, SIDE) * SIDE + owner // SIDE) * CAP + lax.rem(to_row, CAP)
    from_row = lax.broadcasted_iota(jnp.int32, (ROWS, ROWS), 1)
    turn[...] = jnp.where(from_row == source[:, :1], 1.0, 0.0).astype(bf16)
    for copy in i_copies:
        copy.wait()
    t_to = lax.broadcasted_iota(jnp.int32, (LINE, LINE), 0)
    t_from = lax.broadcasted_iota(jnp.int32, (LINE, LINE), 1)
    before = jnp.where((t_from < t_to) & (t_from // TOK == t_to // TOK), 1.0, 0.0).astype(bf16)
    base = ((lax.broadcasted_iota(jnp.int32, (LINE, HD), 0) // TOK) * CAP).astype(jnp.float32)
    lane = lax.broadcasted_iota(jnp.int32, (LINE, HD), 1)
    slot = lax.broadcasted_iota(jnp.int32, (LINE, LINE), 1).astype(jnp.float32)
    slot_t = lax.broadcasted_iota(jnp.int32, (PACK, LINE), 0).astype(jnp.float32)
    for half in range(2):
        owners = [yy * SIDE + i if half == 0 else i * SIDE + zz for i in range(SIDE)]
        ids = jnp.concatenate([ids_all[owner] for owner in owners], axis=0)
        chosen = functools.reduce(jnp.logical_or, [ids[:, j : j + 1] == lane for j in range(6)])
        rank = mm(before, jnp.where(chosen, 1.0, 0.0).astype(bf16))
        place = jnp.where(chosen, base + rank, -1.0)
        place_t[half] = jnp.transpose(place)
        for d in range(SIDE):
            expert = along(seconds[half], d)
            column = jnp.sum(jnp.where(lane == expert, place, 0.0), axis=1, keepdims=True)
            packs[half, d] = jnp.where(slot == column, 1.0, 0.0).astype(bf16)

    for copy in x_copies:
        copy.wait()
    parts = [lse0_ref[0]] + [lse_in[d] for d in range(CHIPS - 1)]
    top = functools.reduce(jnp.maximum, parts)
    weights = [jnp.exp2(part - top) for part in parts]
    total = functools.reduce(jnp.add, weights)
    columns = [jnp.transpose(weight / total) for weight in weights]
    for g in range(CHUNK // HD):
        rows = pl.ds(g * HD, HD)
        mixed = columns[0][:, g : g + 1] * o0_ref[0, rows, :].astype(jnp.float32)
        for d in range(CHIPS - 1):
            mixed += columns[d + 1][:, g : g + 1] * o_in[d, rows, :].astype(jnp.float32)
        att[2 * g] = mixed[:TOK].astype(bf16)
        att[2 * g + 1] = mixed[TOK:].astype(bf16)
    a_copies = []
    for d in range(1, EXPERTS):
        to = lax.rem(me + d, EXPERTS)
        a_copies.append(
            remote(att.at[to], heads.at[me], a_send.at[d - 1], a_recv.at[d - 1], (ctx, to))
        )
    heads[me] = att[me]

    loads[0].wait()
    for copy in a_copies:
        copy.wait()
    joined = jnp.concatenate([heads[h] for h in range(EXPERTS)], axis=1)

    @pl.loop(0, width // STEP)
    def _(c):
        cols = pl.ds(pl.multiple_of(c * STEP, STEP), STEP)
        wide[:, cols] = hid_ref[:, cols].astype(jnp.float32) + mm(joined, proj[:, cols])

    residual = wide[...].astype(bf16).astype(jnp.float32)
    wide[...] = residual
    square = jnp.mean(residual * residual, axis=1, keepdims=True)
    normed = (residual * lax.rsqrt(square + NORM_EPS) * gain_ref[...]).astype(bf16)

    l_copies = {}
    for part in range(PARTS):
        for half in range(2):
            start = half * HALF + part * PART
            line[half, part, at_first[half]] = normed[:, start : start + PART]
            view = line.at[half, part, at_first[half]]
            for d in (2, 1, 3):
                l_copies[half, part, d] = remote(
                    view, view, l_send.at[half, part, d - 1], l_recv.at[half, part, d - 1],
                    (ctx, along(firsts[half], d)),
                )
    affinity = jax.nn.sigmoid(nt(normed, router_ref[...]))
    expert_lane = lax.broadcasted_iota(jnp.int32, affinity.shape, 1)
    chosen = functools.reduce(
        jnp.logical_or, [own_ids[:, j : j + 1] == expert_lane for j in range(6)]
    )
    picked = jnp.where(chosen, affinity, 0.0)
    mix = ROUTE_SCALE * picked / jnp.sum(picked, axis=1, keepdims=True)
    for half in range(2):
        mixes[half, at_first[half]] = jnp.zeros((TOK, HD), jnp.float32)
        mixes[half, at_first[half], :, :EXPERTS] = mix
    p_copies = {}
    for part in range(PARTS):
        for half in range(2):
            for d in (1, 3, 2):
                l_copies[half, part, d].wait_recv()
            mine = pl.ds(pl.multiple_of(at_second[half] * PACK, PACK), PACK)
            tokens = jnp.concatenate([line[half, part, i] for i in range(SIDE)], axis=0)
            for d in (2, 1, 3, 0):
                expert = along(seconds[half], d)
                row = place_t[half, pl.ds(expert, 1), :]
                rows = mm(jnp.where(slot_t == row, 1.0, 0.0).astype(bf16), tokens).astype(bf16)
                if d == 0:
                    pick_in[half, part, mine, :] = rows
                else:
                    pick_out[half, part, d - 1] = rows
                    p_copies[half, part, d] = remote(
                        pick_out.at[half, part, d - 1], pick_in.at[half, part, mine],
                        p_send.at[half, part, d - 1], p_recv.at[half, part, d - 1], (ctx, expert),
                    )
    m_copies = []
    for half in range(2):
        for d in (2, 1, 3):
            view = mixes.at[half, at_first[half]]
            m_copies.append(
                remote(
                    view, view, m_send.at[half, d - 1], m_recv.at[half, d - 1],
                    (ctx, along(firsts[half], d)),
                )
            )
    loads[1].wait()
    loads[2].wait()
    units = gate.shape[1]
    for part in range(PARTS):
        for half in (1, 0):
            for d in (1, 3, 2):
                p_copies[half, part, d].wait_recv()
            if half == 1:
                x_turned[...] = mm(turn[...], pick_in[1, part]).astype(bf16)
        low = pl.ds(part * PART, PART)
        high = pl.ds(HALF + part * PART, PART)
        for start in range(0, units, STEP):
            cols = slice(start, min(start + STEP, units))
            gated = mm(pick_in[0, part], gate[low, cols]) + mm(x_turned[...], gate[high, cols])
            raised = mm(pick_in[0, part], up[low, cols]) + mm(x_turned[...], up[high, cols])
            if part > 0:
                gated += sums[0, :, cols]
                raised += sums[1, :, cols]
            if part < PARTS - 1:
                sums[0, :, cols] = gated
                sums[1, :, cols] = raised
            else:
                inner[:, cols] = (gated / (1.0 + jnp.exp(-gated)) * raised).astype(bf16)
    turned[...] = mm(turn[...], inner[...]).astype(bf16)
    loads[3].wait()
    r_copies = {}
    for part in range(BACKS):
        for half in range(2):
            rows_in = inner if half == 0 else turned

            @pl.loop(0, BACK // STEP)
            def _(c):
                cols = pl.ds(pl.multiple_of(c * STEP, STEP), STEP)
                from_cols = pl.ds(pl.multiple_of(half * HALF + part * BACK + c * STEP, STEP), STEP)
                y_out[half, part, :, cols] = mm(rows_in[...], down[:, from_cols]).astype(bf16)

            for d in (2, 1, 3):
                to = lax.rem(at_second[half] + d, SIDE)
                r_copies[half, part, 0, d] = remote(
                    y_out.at[half, part, pl.ds(pl.multiple_of(to * PACK, PACK), PACK)],
                    y_in.at[half, part, d - 1],
                    r_send.at[half, part, 0, d - 1], r_recv.at[half, part, 0, d - 1],
                    (ctx, along(seconds[half], d)),
                )

    for copy in m_copies:
        copy.wait_recv()
    for part in range(BACKS):
        for half in range(2):
            here = at_second[half]
            share_of = jnp.concatenate([mixes[half, i] for i in range(SIDE)], axis=0)
            summed = jnp.zeros((LINE, BACK), jnp.float32)
            for d in (0, 1, 3, 2):
                back = (SIDE - d) % SIDE
                expert = along(seconds[half], back)
                column = jnp.sum(jnp.where(lane == expert, share_of, 0.0), axis=1, keepdims=True)
                if d == 0:
                    rows = y_out[half, part, pl.ds(pl.multiple_of(here * PACK, PACK), PACK), :]
                else:
                    r_copies[half, part, 0, d].wait_recv()
                    rows = y_in[half, part, d - 1]
                summed += column * mm(packs[half, back][:, :PACK], rows)
            for i in range(SIDE):
                z_out[half, part, i] = summed[i * TOK : (i + 1) * TOK].astype(bf16)
            for d in (2, 1, 3):
                r_copies[half, part, 1, d] = remote(
                    z_out.at[half, part, lax.rem(at_first[half] + d, SIDE)],
                    z_in.at[half, part, d - 1],
                    r_send.at[half, part, 1, d - 1], r_recv.at[half, part, 1, d - 1],
                    (ctx, along(firsts[half], d)),
                )
    for part in range(BACKS):
        for half in range(2):
            start = half * HALF + part * BACK
            cols = slice(start, start + BACK)
            result = wide[:, cols] + z_out[half, part, at_first[half]].astype(jnp.float32)
            for d in (1, 3, 2):
                r_copies[half, part, 1, d].wait_recv()
                result += z_in[half, part, d - 1].astype(jnp.float32)
            out_ref[:, cols] = result.astype(bf16)
    for group in (l_copies, p_copies, r_copies):
        for copy in group.values():
            copy.wait_send()
    for copy in m_copies:
        copy.wait_send()


def post(o0, o, lse0, lse, hidden_in, ids_t, gain, router_t, proj, w_gate, w_up, w_down):
    width = hidden_in.shape[1]
    units = w_gate.shape[1]
    anywhere = pl.BlockSpec(memory_space=pl.ANY)
    vmem = pl.BlockSpec(memory_space=pltpu.VMEM)
    bf16 = jnp.bfloat16
    f32 = jnp.float32
    dma = pltpu.SemaphoreType.DMA
    others = SIDE - 1
    return pl.pallas_call(
        post_kernel,
        out_shape=jax.ShapeDtypeStruct((TOK, width), bf16),
        in_specs=[vmem] * 8 + [anywhere] * 4,
        out_specs=vmem,
        scratch_shapes=[
            pltpu.VMEM((CHIPS - 1, CHUNK, HD), bf16),
            pltpu.VMEM((CHIPS - 1, CHUNK // HD, HD), f32),
            pltpu.VMEM((EXPERTS, TOK, HD), jnp.int32),
            pltpu.VMEM((EXPERTS, TOK, HD), bf16),
            pltpu.VMEM((EXPERTS, TOK, HD), bf16),
            pltpu.VMEM((width, width), bf16),
            pltpu.VMEM((width, units), bf16),
            pltpu.VMEM((width, units), bf16),
            pltpu.VMEM((units, width), bf16),
            pltpu.VMEM((TOK, width), f32),
            pltpu.VMEM((2, SIDE, LINE, LINE), bf16),
            pltpu.VMEM((2, HD, LINE), f32),
            pltpu.VMEM((ROWS, ROWS), bf16),
            pltpu.VMEM((2, PARTS, SIDE, TOK, PART), bf16),
            pltpu.VMEM((2, SIDE, TOK, HD), f32),
            pltpu.VMEM((2, PARTS, others, PACK, PART), bf16),
            pltpu.VMEM((2, PARTS, ROWS, PART), bf16),
            pltpu.VMEM((ROWS, PART), bf16),
            pltpu.VMEM((2, ROWS, units), f32),
            pltpu.VMEM((ROWS, units), bf16),
            pltpu.VMEM((ROWS, units), bf16),
            pltpu.VMEM((2, BACKS, ROWS, BACK), bf16),
            pltpu.VMEM((2, BACKS, others, PACK, BACK), bf16),
            pltpu.VMEM((2, BACKS, SIDE, TOK, BACK), bf16),
            pltpu.VMEM((2, BACKS, others, TOK, BACK), bf16),
            dma((4,)),
            dma((2, CHIPS - 1)),
            dma((2, CHIPS - 1)),
            dma((EXPERTS - 1,)),
            dma((EXPERTS - 1,)),
            dma((EXPERTS - 1,)),
            dma((EXPERTS - 1,)),
            dma((2, PARTS, others)),
            dma((2, PARTS, others)),
            dma((2, others)),
            dma((2, others)),
            dma((2, PARTS, others)),
            dma((2, PARTS, others)),
            dma((2, BACKS, 2, others)),
            dma((2, BACKS, 2, others)),
        ],
        compiler_params=pltpu.CompilerParams(
            collective_id=1, has_side_effects=True, vmem_limit_bytes=62 * MIB
        ),
        name="post",
    )(o0, o, lse0, lse, hidden_in, ids_t, gain, router_t, proj, w_gate, w_up, w_down)


def local(
    hidden_in, queries, keys, values, block_choice, out_proj, norm_gain, router, expert_ids,
    w_gate, w_up, w_down,
):
    width = hidden_in.shape[1]
    proj_all = lax.all_gather(out_proj, "exp", axis=0, tiled=True)
    devices = range(2 * CHIPS)
    swap = [(i, i ^ 1) for i in devices]
    k_oth = lax.ppermute(keys, "ctx", swap)
    v_oth = lax.ppermute(values, "ctx", swap)
    q_from = [
        lax.ppermute(queries, "ctx", [(i, (i - 2 * d) % (2 * CHIPS)) for i in devices])
        for d in range(1, CHIPS)
    ]
    blocks = (keys, k_oth, values, v_oth)
    choice = block_choice.T
    o0, lse0 = attend((0,), choice, (queries,), *blocks)
    o0, *q_from = lax.optimization_barrier((o0, *q_from))
    o, lse = attend((1, 2, 3), choice, q_from, *blocks)
    return post(
        o0, o, lse0, lse, hidden_in, expert_ids.T, norm_gain.reshape(1, width), router.T,
        proj_all, w_gate[0], w_up[0], w_down[0],
    )


def solution(mesh):
    placed = (
        P(("ctx", "exp"), None),
        P("ctx", "exp"),
        P("ctx", "exp"),
        P("ctx", "exp"),
        P(),
        P("exp", None),
        P(),
        P(),
        P(("ctx", "exp"), None),
        P("exp", None, None),
        P("exp", None, None),
        P("exp", None, None),
    )
    return jax.shard_map(
        local, mesh=mesh, in_specs=placed, out_specs=P(("ctx", "exp"), None), check_vma=False
    )
```

```python
import functools

import jax
import jax.numpy as jnp
from jax import lax
from jax.experimental import pallas as pl
from jax.experimental.pallas import tpu as pltpu
from jax.sharding import PartitionSpec as P

HD = 128
BLK = 4096
ROUTE_SCALE = 2.446
NORM_EPS = 1e-06
LOG2E = 1.4426950408889634
LOW = -1e30
JUMP = 100.0
MESH = pl.DeviceIdType.MESH
MIB = 2**20

CHUNK = 1024
TQ = 512
SUB = 128
TKS = 1024
CHIPS = 4
SLOTS = 4
CAP = 36
TOK = 64
EXPERTS = 16
GROUP = EXPERTS * TOK


def nt(a, b):
    return lax.dot_general(a, b, (((1,), (1,)), ((), ())), preferred_element_type=jnp.float32)


def mm(a, b):
    return jnp.dot(a, b, preferred_element_type=jnp.float32)


def attention_kernel(rels, *refs):
    n = len(rels)
    choice, *q_hbm = refs[: 1 + n]
    k_own, k_oth, v_own, v_oth, o_ref, lse_ref = refs[1 + n : 7 + n]
    q_s, k_all, v_all, acc, m_s, l_s, r_s, mx_s, fresh, sems, q_sems = refs[7 + n :]
    scale = HD**-0.5 * LOG2E
    ctx = lax.axis_index("ctx")
    chip = ctx // 2
    core = lax.rem(ctx, 2)
    other = ctx + 1 - 2 * core
    q_copies = [
        pltpu.make_async_copy(q, q_s.at[pl.ds(i * CHUNK, CHUNK)], q_sems.at[i])
        for i, q in enumerate(q_hbm)
    ]
    for copy in q_copies:
        copy.start()
    for slot in range(SLOTS):
        src_k, src_v = (k_own, v_own) if slot < 2 else (k_oth, v_oth)
        src = pl.ds((slot % 2) * BLK, BLK)
        dst = pl.ds(slot * BLK, BLK)
        pltpu.make_async_copy(src_k.at[src], k_all.at[dst], sems.at[0, slot]).start()
        pltpu.make_async_copy(src_v.at[src], v_all.at[dst], sems.at[1, slot]).start()
    for copy in q_copies:
        copy.wait()
    ones = jnp.ones((BLK, HD), jnp.bfloat16)

    def queries(q0, i):
        return q_s[pl.ds(pl.multiple_of(q0 + i * SUB, SUB), SUB), :]

    def masked(s, first_key, first_query):
        key = first_key + lax.broadcasted_iota(jnp.int32, s.shape, 1)
        query = first_query + lax.broadcasted_iota(jnp.int32, s.shape, 0)
        return jnp.where(key <= query, s, LOW)

    def careful(q0, slot, first_key, steps, reach):
        @pl.loop(0, steps)
        def _(step):
            start = first_key + step * TKS
            at = pl.ds(pl.multiple_of(slot * BLK + start, TKS), TKS)
            for i in range(TQ // SUB):
                rows = pl.ds(i * SUB, SUB)
                s = masked(nt(queries(q0, i), k_all[at, :]) * scale, start, reach + i * SUB)
                old = m_s[rows]
                new = jnp.maximum(old, jnp.max(s, axis=1, keepdims=True))
                fade = jnp.exp2(old - new)
                p = jnp.exp2(s - new[:, :1])
                m_s[rows] = new
                l_s[rows] = l_s[rows] * fade + jnp.sum(p, axis=1, keepdims=True)
                acc[rows] = acc[rows] * fade + mm(p.astype(jnp.bfloat16), v_all[at, :])

    def quick(q0, slot, first_key, size, reach, mask):
        base = pl.multiple_of(slot * BLK + first_key, size)
        keys = k_all[pl.ds(base, size), :]
        vals = jnp.concatenate([v_all[pl.ds(base, size), :], ones[:size]], axis=1)
        for i in range(TQ // SUB):
            rows = pl.ds(i * SUB, SUB)
            s = nt(queries(q0, i), keys)
            if mask:
                s = masked(s, first_key, reach + i * SUB)
            old = m_s[rows]
            mx_s[rows] = jnp.broadcast_to(jnp.max(s, axis=1, keepdims=True) * scale, old.shape)
            p = jnp.exp2(s * scale - old[:, :1])
            r_s[rows] = mm(p.astype(jnp.bfloat16), vals)
        jump = jnp.max(mx_s[...] - m_s[...])

        @pl.when(jump <= JUMP)
        def _():
            old = m_s[...]
            new = jnp.maximum(old, mx_s[...])
            fade = jnp.exp2(old - new)
            m_s[...] = new
            acc[...] = (acc[...] + r_s[:, :HD]) * fade
            l_s[...] = (l_s[...] + r_s[:, HD:]) * fade

        @pl.when(jnp.logical_not(jump <= JUMP))
        def _():
            careful(q0, slot, first_key, size // TKS, reach)

    @pl.loop(0, n * CHUNK // TQ)
    def _(tile):
        q0 = pl.multiple_of(tile * TQ, TQ)
        chunk = lax.rem(chip + rels[0] + tile // (CHUNK // TQ), CHIPS)
        row = 14 + chunk // 2
        in_block = lax.rem(2 * chunk + core, 4) * CHUNK + lax.rem(tile, CHUNK // TQ) * TQ
        acc[...] = jnp.zeros_like(acc)
        l_s[...] = jnp.zeros_like(l_s)
        fresh[0] = 1

        @pl.loop(0, SLOTS)
        def _(slot):
            @pl.when(tile == 0)
            def _():
                at = pl.ds(pl.multiple_of(slot * BLK, BLK), BLK)
                first = pl.ds(0, BLK)
                pltpu.make_async_copy(k_own.at[first], k_all.at[at], sems.at[0, slot]).wait()
                pltpu.make_async_copy(v_own.at[first], v_all.at[at], sems.at[1, slot]).wait()

            block = jnp.where(slot < 2, 2 * ctx + slot, 2 * other + slot - 2)
            hit = choice[1, row] == block
            for j in range(2, 8):
                hit = jnp.logical_or(hit, choice[j, row] == block)
            own = block == row
            reach = jnp.where(own, in_block, BLK)

            @pl.when(jnp.logical_and(fresh[0] == 1, jnp.logical_or(own, hit)))
            def _():
                some = k_all[pl.ds(pl.multiple_of(slot * BLK, BLK), 256), :]
                s = masked(nt(q_s[pl.ds(q0, TQ), :], some) * scale, 0, reach)
                m_s[...] = jnp.broadcast_to(jnp.max(s, axis=1, keepdims=True), m_s.shape)
                fresh[0] = 0

            @pl.when(own)
            def _():
                last = in_block // TKS

                @pl.loop(0, last)
                def _(step):
                    quick(q0, slot, pl.multiple_of(step * TKS, TKS), TKS, reach, False)

                quick(q0, slot, pl.multiple_of(last * TKS, TKS), TKS, reach, True)

            @pl.when(jnp.logical_and(hit, jnp.logical_not(own)))
            def _():
                quick(q0, slot, 0, BLK, reach, False)

        total = l_s[...]
        some = total > 0.0
        total = jnp.where(some, total, 1.0)
        o_ref[pl.ds(q0, TQ), :] = (acc[...] / total).astype(jnp.bfloat16)
        lse = jnp.where(some, m_s[...] + jnp.log2(total), LOW)
        flat = jnp.transpose(lse)
        for i in range(TQ // HD):
            lse_ref[pl.ds(tile * (TQ // HD) + i, 1), :] = flat[:1, i * HD : (i + 1) * HD]


def attend(rels, choice, q_parts, k_own, k_oth, v_own, v_oth):
    n = len(rels)
    rows = n * CHUNK
    anywhere = pl.BlockSpec(memory_space=pl.ANY)
    vmem = pl.BlockSpec(memory_space=pltpu.VMEM)
    o, lse = pl.pallas_call(
        functools.partial(attention_kernel, rels),
        out_shape=[
            jax.ShapeDtypeStruct((rows, HD), jnp.bfloat16),
            jax.ShapeDtypeStruct((rows // HD, HD), jnp.float32),
        ],
        in_specs=[pl.BlockSpec(memory_space=pltpu.SMEM)] + [anywhere] * (4 + n),
        out_specs=[vmem, vmem],
        scratch_shapes=[
            pltpu.VMEM((rows, HD), jnp.bfloat16),
            pltpu.VMEM((SLOTS * BLK, HD), jnp.bfloat16),
            pltpu.VMEM((SLOTS * BLK, HD), jnp.bfloat16),
            pltpu.VMEM((TQ, HD), jnp.float32),
            pltpu.VMEM((TQ, HD), jnp.float32),
            pltpu.VMEM((TQ, HD), jnp.float32),
            pltpu.VMEM((TQ, 2 * HD), jnp.float32),
            pltpu.VMEM((TQ, HD), jnp.float32),
            pltpu.SMEM((1,), jnp.int32),
            pltpu.SemaphoreType.DMA((2, SLOTS)),
            pltpu.SemaphoreType.DMA((n,)),
        ],
        compiler_params=pltpu.CompilerParams(vmem_limit_bytes=60 * MIB),
        cost_estimate=pl.CostEstimate(
            flops=2 * 2 * rows * 2 * BLK * 2 * HD, bytes_accessed=10 * MIB, transcendentals=0
        ),
        name="attention_" + "_".join(str(rel) for rel in rels),
    )(choice, *q_parts, k_own, k_oth, v_own, v_oth)
    return o.reshape(n, CHUNK, HD), lse.reshape(n, CHUNK // HD, HD)


SIDE = 4
PACK = SIDE * CAP
LINE = SIDE * TOK
ROWS = EXPERTS * CAP
HALF = 1024
PART = 512
PARTS = HALF // PART
BACK = 512
BACKS = HALF // BACK
STEP = 256


def post_kernel(
    o0_ref, o_ref, lse0_ref, lse_ref, hid_ref, ids_ref, gain_ref, router_ref,
    proj_hbm, gate_hbm, up_hbm, down_hbm,
    out_ref,
    o_in, lse_in, mixing, ids_all, att, heads, proj, gate, up, down, wide, packs, place_t, turn,
    line, mixes, pick_out, pick_in, x_turned, sums, inner, turned, y_out, y_in, z_out, z_in,
    near, w_send, w_recv, x_send, x_recv, i_send, i_recv, a_send, a_recv, l_send, l_recv, m_send, m_recv,
    p_send, p_recv, r_send, r_recv,
):
    ctx = lax.axis_index("ctx")
    me = lax.axis_index("exp")
    chip = ctx // 2
    core = lax.rem(ctx, 2)
    yy = me // SIDE
    zz = lax.rem(me, SIDE)
    width = hid_ref.shape[1]
    bf16 = jnp.bfloat16

    def along(axis, d):
        if axis == 0:
            return lax.rem(yy + d, SIDE) * SIDE + zz
        return yy * SIDE + lax.rem(zz + d, SIDE)

    firsts = (1, 0)
    seconds = (0, 1)
    at_first = (zz, yy)
    at_second = (yy, zz)

    loads = [
        pltpu.make_async_copy(src, dst, near.at[i])
        for i, (src, dst) in enumerate(
            ((proj_hbm, proj), (gate_hbm, gate), (up_hbm, up), (down_hbm, down))
        )
    ]
    for load in loads:
        load.start()
    barrier = pltpu.get_barrier_semaphore()
    for d in range(1, CHIPS):
        peer = (2 * lax.rem(chip + d, CHIPS) + core, me)
        pl.semaphore_signal(barrier, inc=1, device_id=peer, device_id_type=MESH)
    for d in range(1, EXPERTS):
        peer = (ctx, lax.rem(me + d, EXPERTS))
        pl.semaphore_signal(barrier, inc=1, device_id=peer, device_id_type=MESH)
    ids_all[me] = jnp.full((TOK, HD), -1, jnp.int32)
    own_ids = jnp.transpose(ids_ref[...].astype(jnp.float32)).astype(jnp.int32)
    ids_all[me, :, :6] = own_ids
    pl.semaphore_wait(barrier, CHIPS - 1 + EXPERTS - 1)

    def remote(src, dst, send, recv, peer):
        copy = pltpu.make_async_remote_copy(
            src_ref=src, dst_ref=dst, send_sem=send, recv_sem=recv,
            device_id=peer, device_id_type=MESH,
        )
        copy.start()
        return copy

    i_copies = []
    for d in range(1, EXPERTS):
        peer = (ctx, lax.rem(me + d, EXPERTS))
        i_copies.append(
            remote(ids_all.at[me], ids_all.at[me], i_send.at[d - 1], i_recv.at[d - 1], peer)
        )
    w_copies = [
        remote(
            lse_ref.at[d - 1], lse_in.at[d - 1], w_send.at[d - 1], w_recv.at[d - 1],
            (2 * lax.rem(chip + d, CHIPS) + core, me),
        )
        for d in (2, 1, 3)
    ]
    x_copies = {}
    for k in range(SIDE):
        rows = pl.ds(pl.multiple_of(lax.rem(yy + k, SIDE) * LINE, LINE), LINE)
        for d in (2, 1, 3):
            x_copies[k, d] = remote(
                o_ref.at[d - 1, rows], o_in.at[d - 1, rows], x_send.at[k, d - 1],
                x_recv.at[k, d - 1], (2 * lax.rem(chip + d, CHIPS) + core, me),
            )
    to_row = lax.broadcasted_iota(jnp.int32, (ROWS, HD), 0)
    owner = to_row // CAP
    source = (lax.rem(owner, SIDE) * SIDE + owner // SIDE) * CAP + lax.rem(to_row, CAP)
    from_row = lax.broadcasted_iota(jnp.int32, (ROWS, ROWS), 1)
    turn[...] = jnp.where(from_row == source[:, :1], 1.0, 0.0).astype(bf16)
    t_to = lax.broadcasted_iota(jnp.int32, (LINE, LINE), 0)
    t_from = lax.broadcasted_iota(jnp.int32, (LINE, LINE), 1)
    before = jnp.where((t_from < t_to) & (t_from // TOK == t_to // TOK), 1.0, 0.0).astype(bf16)
    base = ((lax.broadcasted_iota(jnp.int32, (LINE, HD), 0) // TOK) * CAP).astype(jnp.float32)
    lane = lax.broadcasted_iota(jnp.int32, (LINE, HD), 1)
    slot = lax.broadcasted_iota(jnp.int32, (LINE, LINE), 1).astype(jnp.float32)
    slot_t = lax.broadcasted_iota(jnp.int32, (PACK, LINE), 0).astype(jnp.float32)
    def pack(half):
        owners = [yy * SIDE + i if half == 0 else i * SIDE + zz for i in range(SIDE)]
        ids = jnp.concatenate([ids_all[owner] for owner in owners], axis=0)
        chosen = functools.reduce(jnp.logical_or, [ids[:, j : j + 1] == lane for j in range(6)])
        rank = mm(before, jnp.where(chosen, 1.0, 0.0).astype(bf16))
        place = jnp.where(chosen, base + rank, -1.0)
        place_t[half] = jnp.transpose(place)
        for d in range(SIDE):
            expert = along(seconds[half], d)
            column = jnp.sum(jnp.where(lane == expert, place, 0.0), axis=1, keepdims=True)
            packs[half, d] = jnp.where(slot == column, 1.0, 0.0).astype(bf16)


    for copy in w_copies:
        copy.wait()
    parts = [lse0_ref[0]] + [lse_in[d] for d in range(CHIPS - 1)]
    top = functools.reduce(jnp.maximum, parts)
    weights = [jnp.exp2(part - top) for part in parts]
    total = functools.reduce(jnp.add, weights)
    for d in range(CHIPS):
        column = jnp.transpose(weights[d] / total)
        for g in range(CHUNK // HD):
            mixing[d, g * HD : (g + 1) * HD] = jnp.broadcast_to(column[:, g : g + 1], (HD, HD))
    a_copies = []
    for k in range(SIDE):
        for d in (1, 3, 2):
            x_copies[k, d].wait()
        for i in range(SIDE):
            to = lax.rem(yy + k, SIDE) * SIDE + lax.rem(zz + i, SIDE)
            rows = pl.ds(pl.multiple_of(to * TOK, TOK), TOK)
            mixed = mixing[0, rows, :] * o0_ref[0, rows, :].astype(jnp.float32)
            for d in range(CHIPS - 1):
                mixed += mixing[d + 1, rows, :] * o_in[d, rows, :].astype(jnp.float32)
            if k == 0 and i == 0:
                heads[me] = mixed.astype(bf16)
            else:
                n = k * SIDE + i - 1
                att[to] = mixed.astype(bf16)
                a_copies.append(
                    remote(att.at[to], heads.at[me], a_send.at[n], a_recv.at[n], (ctx, to))
                )
        if k == 0:
            for copy in i_copies:
                copy.wait()
        if k < 2:
            pack(k)

    loads[0].wait()
    for copy in a_copies:
        copy.wait()
    joined = jnp.concatenate([heads[h] for h in range(EXPERTS)], axis=1)

    @pl.loop(0, width // STEP)
    def _(c):
        cols = pl.ds(pl.multiple_of(c * STEP, STEP), STEP)
        wide[:, cols] = hid_ref[:, cols].astype(jnp.float32) + mm(joined, proj[:, cols])

    residual = wide[...].astype(bf16).astype(jnp.float32)
    wide[...] = residual
    square = jnp.mean(residual * residual, axis=1, keepdims=True)
    normed = (residual * lax.rsqrt(square + NORM_EPS) * gain_ref[...]).astype(bf16)

    l_copies = {}
    for part in range(PARTS):
        for half in range(2):
            start = half * HALF + part * PART
            line[half, part, at_first[half]] = normed[:, start : start + PART]
            view = line.at[half, part, at_first[half]]
            for d in (2, 1, 3):
                l_copies[half, part, d] = remote(
                    view, view, l_send.at[half, part, d - 1], l_recv.at[half, part, d - 1],
                    (ctx, along(firsts[half], d)),
                )
    affinity = jax.nn.sigmoid(nt(normed, router_ref[...]))
    expert_lane = lax.broadcasted_iota(jnp.int32, affinity.shape, 1)
    chosen = functools.reduce(
        jnp.logical_or, [own_ids[:, j : j + 1] == expert_lane for j in range(6)]
    )
    picked = jnp.where(chosen, affinity, 0.0)
    mix = ROUTE_SCALE * picked / jnp.sum(picked, axis=1, keepdims=True)
    for half in range(2):
        mixes[half, at_first[half]] = jnp.zeros((TOK, HD), jnp.float32)
        mixes[half, at_first[half], :, :EXPERTS] = mix
    p_copies = {}
    for part in range(PARTS):
        for half in range(2):
            for d in (1, 3, 2):
                l_copies[half, part, d].wait_recv()
            mine = pl.ds(pl.multiple_of(at_second[half] * PACK, PACK), PACK)
            tokens = jnp.concatenate([line[half, part, i] for i in range(SIDE)], axis=0)
            for d in (2, 1, 3, 0):
                expert = along(seconds[half], d)
                row = place_t[half, pl.ds(expert, 1), :]
                rows = mm(jnp.where(slot_t == row, 1.0, 0.0).astype(bf16), tokens).astype(bf16)
                if d == 0:
                    pick_in[half, part, mine, :] = rows
                else:
                    pick_out[half, part, d - 1] = rows
                    p_copies[half, part, d] = remote(
                        pick_out.at[half, part, d - 1], pick_in.at[half, part, mine],
                        p_send.at[half, part, d - 1], p_recv.at[half, part, d - 1], (ctx, expert),
                    )
    m_copies = []
    for half in range(2):
        for d in (2, 1, 3):
            view = mixes.at[half, at_first[half]]
            m_copies.append(
                remote(
                    view, view, m_send.at[half, d - 1], m_recv.at[half, d - 1],
                    (ctx, along(firsts[half], d)),
                )
            )
    loads[1].wait()
    loads[2].wait()
    units = gate.shape[1]
    for part in range(PARTS):
        for half in (1, 0):
            for d in (1, 3, 2):
                p_copies[half, part, d].wait_recv()
            if half == 1:
                x_turned[...] = mm(turn[...], pick_in[1, part]).astype(bf16)
        low = pl.ds(part * PART, PART)
        high = pl.ds(HALF + part * PART, PART)
        for start in range(0, units, STEP):
            cols = slice(start, min(start + STEP, units))
            gated = mm(pick_in[0, part], gate[low, cols]) + mm(x_turned[...], gate[high, cols])
            raised = mm(pick_in[0, part], up[low, cols]) + mm(x_turned[...], up[high, cols])
            if part > 0:
                gated += sums[0, :, cols]
                raised += sums[1, :, cols]
            if part < PARTS - 1:
                sums[0, :, cols] = gated
                sums[1, :, cols] = raised
            else:
                inner[:, cols] = (gated / (1.0 + jnp.exp(-gated)) * raised).astype(bf16)
    turned[...] = mm(turn[...], inner[...]).astype(bf16)
    loads[3].wait()
    r_copies = {}
    for part in range(BACKS):
        for half in range(2):
            rows_in = inner if half == 0 else turned

            @pl.loop(0, BACK // STEP)
            def _(c):
                cols = pl.ds(pl.multiple_of(c * STEP, STEP), STEP)
                from_cols = pl.ds(pl.multiple_of(half * HALF + part * BACK + c * STEP, STEP), STEP)
                y_out[half, part, :, cols] = mm(rows_in[...], down[:, from_cols]).astype(bf16)

            for d in (2, 1, 3):
                to = lax.rem(at_second[half] + d, SIDE)
                r_copies[half, part, 0, d] = remote(
                    y_out.at[half, part, pl.ds(pl.multiple_of(to * PACK, PACK), PACK)],
                    y_in.at[half, part, d - 1],
                    r_send.at[half, part, 0, d - 1], r_recv.at[half, part, 0, d - 1],
                    (ctx, along(seconds[half], d)),
                )

    for copy in m_copies:
        copy.wait_recv()
    for part in range(BACKS):
        for half in range(2):
            here = at_second[half]
            share_of = jnp.concatenate([mixes[half, i] for i in range(SIDE)], axis=0)
            summed = jnp.zeros((LINE, BACK), jnp.float32)
            for d in (0, 1, 3, 2):
                back = (SIDE - d) % SIDE
                expert = along(seconds[half], back)
                column = jnp.sum(jnp.where(lane == expert, share_of, 0.0), axis=1, keepdims=True)
                if d == 0:
                    rows = y_out[half, part, pl.ds(pl.multiple_of(here * PACK, PACK), PACK), :]
                else:
                    r_copies[half, part, 0, d].wait_recv()
                    rows = y_in[half, part, d - 1]
                summed += column * mm(packs[half, back][:, :PACK], rows)
            for i in range(SIDE):
                z_out[half, part, i] = summed[i * TOK : (i + 1) * TOK].astype(bf16)
            for d in (2, 1, 3):
                r_copies[half, part, 1, d] = remote(
                    z_out.at[half, part, lax.rem(at_first[half] + d, SIDE)],
                    z_in.at[half, part, d - 1],
                    r_send.at[half, part, 1, d - 1], r_recv.at[half, part, 1, d - 1],
                    (ctx, along(firsts[half], d)),
                )
    for part in range(BACKS):
        for half in range(2):
            start = half * HALF + part * BACK
            cols = slice(start, start + BACK)
            result = wide[:, cols] + z_out[half, part, at_first[half]].astype(jnp.float32)
            for d in (1, 3, 2):
                r_copies[half, part, 1, d].wait_recv()
                result += z_in[half, part, d - 1].astype(jnp.float32)
            out_ref[:, cols] = result.astype(bf16)
    for group in (l_copies, p_copies, r_copies):
        for copy in group.values():
            copy.wait_send()
    for copy in m_copies:
        copy.wait_send()


def post(o0, o, lse0, lse, hidden_in, ids_t, gain, router_t, proj, w_gate, w_up, w_down):
    width = hidden_in.shape[1]
    units = w_gate.shape[1]
    anywhere = pl.BlockSpec(memory_space=pl.ANY)
    vmem = pl.BlockSpec(memory_space=pltpu.VMEM)
    bf16 = jnp.bfloat16
    f32 = jnp.float32
    dma = pltpu.SemaphoreType.DMA
    others = SIDE - 1
    return pl.pallas_call(
        post_kernel,
        out_shape=jax.ShapeDtypeStruct((TOK, width), bf16),
        in_specs=[vmem] * 8 + [anywhere] * 4,
        out_specs=vmem,
        scratch_shapes=[
            pltpu.VMEM((CHIPS - 1, CHUNK, HD), bf16),
            pltpu.VMEM((CHIPS - 1, CHUNK // HD, HD), f32),
            pltpu.VMEM((CHIPS, CHUNK, HD), f32),
            pltpu.VMEM((EXPERTS, TOK, HD), jnp.int32),
            pltpu.VMEM((EXPERTS, TOK, HD), bf16),
            pltpu.VMEM((EXPERTS, TOK, HD), bf16),
            pltpu.VMEM((width, width), bf16),
            pltpu.VMEM((width, units), bf16),
            pltpu.VMEM((width, units), bf16),
            pltpu.VMEM((units, width), bf16),
            pltpu.VMEM((TOK, width), f32),
            pltpu.VMEM((2, SIDE, LINE, LINE), bf16),
            pltpu.VMEM((2, HD, LINE), f32),
            pltpu.VMEM((ROWS, ROWS), bf16),
            pltpu.VMEM((2, PARTS, SIDE, TOK, PART), bf16),
            pltpu.VMEM((2, SIDE, TOK, HD), f32),
            pltpu.VMEM((2, PARTS, others, PACK, PART), bf16),
            pltpu.VMEM((2, PARTS, ROWS, PART), bf16),
            pltpu.VMEM((ROWS, PART), bf16),
            pltpu.VMEM((2, ROWS, units), f32),
            pltpu.VMEM((ROWS, units), bf16),
            pltpu.VMEM((ROWS, units), bf16),
            pltpu.VMEM((2, BACKS, ROWS, BACK), bf16),
            pltpu.VMEM((2, BACKS, others, PACK, BACK), bf16),
            pltpu.VMEM((2, BACKS, SIDE, TOK, BACK), bf16),
            pltpu.VMEM((2, BACKS, others, TOK, BACK), bf16),
            dma((4,)),
            dma((CHIPS - 1,)),
            dma((CHIPS - 1,)),
            dma((SIDE, CHIPS - 1)),
            dma((SIDE, CHIPS - 1)),
            dma((EXPERTS - 1,)),
            dma((EXPERTS - 1,)),
            dma((EXPERTS - 1,)),
            dma((EXPERTS - 1,)),
            dma((2, PARTS, others)),
            dma((2, PARTS, others)),
            dma((2, others)),
            dma((2, others)),
            dma((2, PARTS, others)),
            dma((2, PARTS, others)),
            dma((2, BACKS, 2, others)),
            dma((2, BACKS, 2, others)),
        ],
        compiler_params=pltpu.CompilerParams(
            collective_id=1, has_side_effects=True, vmem_limit_bytes=62 * MIB
        ),
        name="post",
    )(o0, o, lse0, lse, hidden_in, ids_t, gain, router_t, proj, w_gate, w_up, w_down)


def local(
    hidden_in, queries, keys, values, block_choice, out_proj, norm_gain, router, expert_ids,
    w_gate, w_up, w_down,
):
    width = hidden_in.shape[1]
    proj_all = lax.all_gather(out_proj, "exp", axis=0, tiled=True)
    devices = range(2 * CHIPS)
    swap = [(i, i ^ 1) for i in devices]
    k_oth = lax.ppermute(keys, "ctx", swap)
    v_oth = lax.ppermute(values, "ctx", swap)
    q_from = [
        lax.ppermute(queries, "ctx", [(i, (i - 2 * d) % (2 * CHIPS)) for i in devices])
        for d in range(1, CHIPS)
    ]
    blocks = (keys, k_oth, values, v_oth)
    choice = block_choice.T
    o0, lse0 = attend((0,), choice, (queries,), *blocks)
    o0, *q_from = lax.optimization_barrier((o0, *q_from))
    o, lse = attend((1, 2, 3), choice, q_from, *blocks)
    return post(
        o0, o, lse0, lse, hidden_in, expert_ids.T, norm_gain.reshape(1, width), router.T,
        proj_all, w_gate[0], w_up[0], w_down[0],
    )


def solution(mesh):
    placed = (
        P(("ctx", "exp"), None),
        P("ctx", "exp"),
        P("ctx", "exp"),
        P("ctx", "exp"),
        P(),
        P("exp", None),
        P(),
        P(),
        P(("ctx", "exp"), None),
        P("exp", None, None),
        P("exp", None, None),
        P("exp", None, None),
    )
    return jax.shard_map(
        local, mesh=mesh, in_specs=placed, out_specs=P(("ctx", "exp"), None), check_vma=False
    )
```

```python
import functools

import jax
import jax.numpy as jnp
from jax import lax
from jax.experimental import pallas as pl
from jax.experimental.pallas import tpu as pltpu
from jax.sharding import PartitionSpec as P

HD = 128
BLK = 4096
ROUTE_SCALE = 2.446
NORM_EPS = 1e-06
LOG2E = 1.4426950408889634
LOW = -1e30
JUMP = 100.0
MESH = pl.DeviceIdType.MESH
MIB = 2**20

CHUNK = 1024
TQ = 1024
SUB = 128
TKS = 1024
CHIPS = 4
SLOTS = 4
CAP = 36
TOK = 64
EXPERTS = 16
GROUP = EXPERTS * TOK


def nt(a, b):
    return lax.dot_general(a, b, (((1,), (1,)), ((), ())), preferred_element_type=jnp.float32)


def mm(a, b):
    return jnp.dot(a, b, preferred_element_type=jnp.float32)


def attention_kernel(rels, *refs):
    n = len(rels)
    choice, *q_hbm = refs[: 1 + n]
    k_own, k_oth, v_own, v_oth, o_ref, lse_ref = refs[1 + n : 7 + n]
    q_s, k_all, v_all, acc, m_s, l_s, r_s, mx_s, fresh, sems, q_sems = refs[7 + n :]
    scale = HD**-0.5 * LOG2E
    ctx = lax.axis_index("ctx")
    chip = ctx // 2
    core = lax.rem(ctx, 2)
    other = ctx + 1 - 2 * core
    q_copies = [
        pltpu.make_async_copy(q, q_s.at[pl.ds(i * CHUNK, CHUNK)], q_sems.at[i])
        for i, q in enumerate(q_hbm)
    ]
    for copy in q_copies:
        copy.start()
    for slot in range(SLOTS):
        src_k, src_v = (k_own, v_own) if slot < 2 else (k_oth, v_oth)
        src = pl.ds((slot % 2) * BLK, BLK)
        dst = pl.ds(slot * BLK, BLK)
        pltpu.make_async_copy(src_k.at[src], k_all.at[dst], sems.at[0, slot]).start()
        pltpu.make_async_copy(src_v.at[src], v_all.at[dst], sems.at[1, slot]).start()
    for copy in q_copies:
        copy.wait()
    ones = jnp.ones((BLK, HD), jnp.bfloat16)

    def queries(q0, i):
        return q_s[pl.ds(pl.multiple_of(q0 + i * SUB, SUB), SUB), :]

    def masked(s, first_key, first_query):
        key = first_key + lax.broadcasted_iota(jnp.int32, s.shape, 1)
        query = first_query + lax.broadcasted_iota(jnp.int32, s.shape, 0)
        return jnp.where(key <= query, s, LOW)

    def careful(q0, slot, first_key, steps, reach):
        @pl.loop(0, steps)
        def _(step):
            start = first_key + step * TKS
            at = pl.ds(pl.multiple_of(slot * BLK + start, TKS), TKS)

            @pl.loop(0, TQ // SUB)
            def _(i):
                rows = pl.ds(pl.multiple_of(i * SUB, SUB), SUB)
                s = masked(nt(queries(q0, i), k_all[at, :]) * scale, start, reach + i * SUB)
                old = m_s[rows]
                new = jnp.maximum(old, jnp.max(s, axis=1, keepdims=True))
                fade = jnp.exp2(old - new)
                p = jnp.exp2(s - new[:, :1])
                m_s[rows] = new
                l_s[rows] = l_s[rows] * fade + jnp.sum(p, axis=1, keepdims=True)
                acc[rows] = acc[rows] * fade + mm(p.astype(jnp.bfloat16), v_all[at, :])

    def quick(q0, slot, first_key, size, reach, mask):
        base = pl.multiple_of(slot * BLK + first_key, size)
        keys = k_all[pl.ds(base, size), :]
        vals = jnp.concatenate([v_all[pl.ds(base, size), :], ones[:size]], axis=1)
        for i in range(TQ // SUB):
            rows = pl.ds(i * SUB, SUB)
            s = nt(queries(q0, i), keys)
            if mask:
                s = masked(s, first_key, reach + i * SUB)
            old = m_s[rows]
            mx_s[rows] = jnp.broadcast_to(jnp.max(s, axis=1, keepdims=True) * scale, old.shape)
            p = jnp.exp2(s * scale - old[:, :1])
            r_s[rows] = mm(p.astype(jnp.bfloat16), vals)
        jump = jnp.max(mx_s[...] - m_s[...])

        @pl.when(jump <= JUMP)
        def _():
            old = m_s[...]
            new = jnp.maximum(old, mx_s[...])
            fade = jnp.exp2(old - new)
            m_s[...] = new
            acc[...] = (acc[...] + r_s[:, :HD]) * fade
            l_s[...] = (l_s[...] + r_s[:, HD:]) * fade

        @pl.when(jnp.logical_not(jump <= JUMP))
        def _():
            careful(q0, slot, first_key, size // TKS, reach)

    @pl.loop(0, n * CHUNK // TQ)
    def _(tile):
        q0 = pl.multiple_of(tile * TQ, TQ)
        chunk = lax.rem(chip + rels[0] + tile // (CHUNK // TQ), CHIPS)
        row = 14 + chunk // 2
        in_block = lax.rem(2 * chunk + core, 4) * CHUNK + lax.rem(tile, CHUNK // TQ) * TQ
        acc[...] = jnp.zeros_like(acc)
        l_s[...] = jnp.zeros_like(l_s)
        fresh[0] = 1

        @pl.loop(0, SLOTS)
        def _(slot):
            @pl.when(tile == 0)
            def _():
                at = pl.ds(pl.multiple_of(slot * BLK, BLK), BLK)
                first = pl.ds(0, BLK)
                pltpu.make_async_copy(k_own.at[first], k_all.at[at], sems.at[0, slot]).wait()
                pltpu.make_async_copy(v_own.at[first], v_all.at[at], sems.at[1, slot]).wait()

            block = jnp.where(slot < 2, 2 * ctx + slot, 2 * other + slot - 2)
            hit = choice[1, row] == block
            for j in range(2, 8):
                hit = jnp.logical_or(hit, choice[j, row] == block)
            own = block == row
            reach = jnp.where(own, in_block, BLK)

            @pl.when(jnp.logical_and(fresh[0] == 1, jnp.logical_or(own, hit)))
            def _():
                some = k_all[pl.ds(pl.multiple_of(slot * BLK, BLK), 256), :]
                s = masked(nt(q_s[pl.ds(q0, TQ), :], some) * scale, 0, reach)
                m_s[...] = jnp.broadcast_to(jnp.max(s, axis=1, keepdims=True), m_s.shape)
                fresh[0] = 0

            @pl.when(own)
            def _():
                @pl.loop(0, in_block // TKS + 1)
                def _(step):
                    quick(q0, slot, pl.multiple_of(step * TKS, TKS), TKS, reach, True)

            @pl.when(jnp.logical_and(hit, jnp.logical_not(own)))
            def _():
                quick(q0, slot, 0, BLK, reach, False)

        total = l_s[...]
        some = total > 0.0
        total = jnp.where(some, total, 1.0)
        o_ref[pl.ds(q0, TQ), :] = (acc[...] / total).astype(jnp.bfloat16)
        lse = jnp.where(some, m_s[...] + jnp.log2(total), LOW)
        flat = jnp.transpose(lse)
        for i in range(TQ // HD):
            lse_ref[pl.ds(tile * (TQ // HD) + i, 1), :] = flat[:1, i * HD : (i + 1) * HD]


def attend(rels, choice, q_parts, k_own, k_oth, v_own, v_oth):
    n = len(rels)
    rows = n * CHUNK
    anywhere = pl.BlockSpec(memory_space=pl.ANY)
    vmem = pl.BlockSpec(memory_space=pltpu.VMEM)
    o, lse = pl.pallas_call(
        functools.partial(attention_kernel, rels),
        out_shape=[
            jax.ShapeDtypeStruct((rows, HD), jnp.bfloat16),
            jax.ShapeDtypeStruct((rows // HD, HD), jnp.float32),
        ],
        in_specs=[pl.BlockSpec(memory_space=pltpu.SMEM)] + [anywhere] * (4 + n),
        out_specs=[vmem, vmem],
        scratch_shapes=[
            pltpu.VMEM((rows, HD), jnp.bfloat16),
            pltpu.VMEM((SLOTS * BLK, HD), jnp.bfloat16),
            pltpu.VMEM((SLOTS * BLK, HD), jnp.bfloat16),
            pltpu.VMEM((TQ, HD), jnp.float32),
            pltpu.VMEM((TQ, HD), jnp.float32),
            pltpu.VMEM((TQ, HD), jnp.float32),
            pltpu.VMEM((TQ, 2 * HD), jnp.float32),
            pltpu.VMEM((TQ, HD), jnp.float32),
            pltpu.SMEM((1,), jnp.int32),
            pltpu.SemaphoreType.DMA((2, SLOTS)),
            pltpu.SemaphoreType.DMA((n,)),
        ],
        compiler_params=pltpu.CompilerParams(vmem_limit_bytes=60 * MIB),
        cost_estimate=pl.CostEstimate(
            flops=2 * 2 * rows * 2 * BLK * 2 * HD, bytes_accessed=10 * MIB, transcendentals=0
        ),
        name="attention_" + "_".join(str(rel) for rel in rels),
    )(choice, *q_parts, k_own, k_oth, v_own, v_oth)
    return o.reshape(n, CHUNK, HD), lse.reshape(n, CHUNK // HD, HD)


SIDE = 4
PACK = SIDE * CAP
LINE = SIDE * TOK
ROWS = EXPERTS * CAP
HALF = 1024
PART = 512
PARTS = HALF // PART
BACK = 512
BACKS = HALF // BACK
STEP = 256


def post_kernel(
    o0_ref, o_ref, lse0_ref, lse_ref, hid_ref, ids_ref, gain_ref, router_ref,
    proj_hbm, gate_hbm, up_hbm, down_hbm,
    out_ref,
    o_in, lse_in, mixing, ids_all, att, heads, proj, gate, up, down, wide, packs, place_t, turn,
    line, mixes, pick_out, pick_in, x_turned, sums, inner, turned, y_out, y_in, z_out, z_in,
    near, w_send, w_recv, x_send, x_recv, i_send, i_recv, a_send, a_recv, l_send, l_recv, m_send, m_recv,
    p_send, p_recv, r_send, r_recv,
):
    ctx = lax.axis_index("ctx")
    me = lax.axis_index("exp")
    chip = ctx // 2
    core = lax.rem(ctx, 2)
    yy = me // SIDE
    zz = lax.rem(me, SIDE)
    width = hid_ref.shape[1]
    bf16 = jnp.bfloat16

    def along(axis, d):
        if axis == 0:
            return lax.rem(yy + d, SIDE) * SIDE + zz
        return yy * SIDE + lax.rem(zz + d, SIDE)

    firsts = (1, 0)
    seconds = (0, 1)
    at_first = (zz, yy)
    at_second = (yy, zz)

    loads = [
        pltpu.make_async_copy(src, dst, near.at[i])
        for i, (src, dst) in enumerate(
            ((proj_hbm, proj), (gate_hbm, gate), (up_hbm, up), (down_hbm, down))
        )
    ]
    for load in loads:
        load.start()
    barrier = pltpu.get_barrier_semaphore()
    for d in range(1, CHIPS):
        peer = (2 * lax.rem(chip + d, CHIPS) + core, me)
        pl.semaphore_signal(barrier, inc=1, device_id=peer, device_id_type=MESH)
    for d in range(1, EXPERTS):
        peer = (ctx, lax.rem(me + d, EXPERTS))
        pl.semaphore_signal(barrier, inc=1, device_id=peer, device_id_type=MESH)
    ids_all[me] = jnp.full((TOK, HD), -1, jnp.int32)
    own_ids = jnp.transpose(ids_ref[...].astype(jnp.float32)).astype(jnp.int32)
    ids_all[me, :, :6] = own_ids
    pl.semaphore_wait(barrier, CHIPS - 1 + EXPERTS - 1)

    def remote(src, dst, send, recv, peer):
        copy = pltpu.make_async_remote_copy(
            src_ref=src, dst_ref=dst, send_sem=send, recv_sem=recv,
            device_id=peer, device_id_type=MESH,
        )
        copy.start()
        return copy

    i_copies = []
    for d in range(1, EXPERTS):
        peer = (ctx, lax.rem(me + d, EXPERTS))
        i_copies.append(
            remote(ids_all.at[me], ids_all.at[me], i_send.at[d - 1], i_recv.at[d - 1], peer)
        )
    w_copies = [
        remote(
            lse_ref.at[d - 1], lse_in.at[d - 1], w_send.at[d - 1], w_recv.at[d - 1],
            (2 * lax.rem(chip + d, CHIPS) + core, me),
        )
        for d in (2, 1, 3)
    ]
    x_copies = {}
    for k in range(SIDE):
        rows = pl.ds(pl.multiple_of(lax.rem(yy + k, SIDE) * LINE, LINE), LINE)
        for d in (2, 1, 3):
            x_copies[k, d] = remote(
                o_ref.at[d - 1, rows], o_in.at[d - 1, rows], x_send.at[k, d - 1],
                x_recv.at[k, d - 1], (2 * lax.rem(chip + d, CHIPS) + core, me),
            )
    to_row = lax.broadcasted_iota(jnp.int32, (ROWS, HD), 0)
    owner = to_row // CAP
    source = (lax.rem(owner, SIDE) * SIDE + owner // SIDE) * CAP + lax.rem(to_row, CAP)
    from_row = lax.broadcasted_iota(jnp.int32, (ROWS, ROWS), 1)
    turn[...] = jnp.where(from_row == source[:, :1], 1.0, 0.0).astype(bf16)
    t_to = lax.broadcasted_iota(jnp.int32, (LINE, LINE), 0)
    t_from = lax.broadcasted_iota(jnp.int32, (LINE, LINE), 1)
    before = jnp.where((t_from < t_to) & (t_from // TOK == t_to // TOK), 1.0, 0.0).astype(bf16)
    base = ((lax.broadcasted_iota(jnp.int32, (LINE, HD), 0) // TOK) * CAP).astype(jnp.float32)
    lane = lax.broadcasted_iota(jnp.int32, (LINE, HD), 1)
    slot = lax.broadcasted_iota(jnp.int32, (LINE, LINE), 1).astype(jnp.float32)
    slot_t = lax.broadcasted_iota(jnp.int32, (PACK, LINE), 0).astype(jnp.float32)
    def pack(half):
        owners = [yy * SIDE + i if half == 0 else i * SIDE + zz for i in range(SIDE)]
        ids = jnp.concatenate([ids_all[owner] for owner in owners], axis=0)
        chosen = functools.reduce(jnp.logical_or, [ids[:, j : j + 1] == lane for j in range(6)])
        rank = mm(before, jnp.where(chosen, 1.0, 0.0).astype(bf16))
        place = jnp.where(chosen, base + rank, -1.0)
        place_t[half] = jnp.transpose(place)
        for d in range(SIDE):
            expert = along(seconds[half], d)
            column = jnp.sum(jnp.where(lane == expert, place, 0.0), axis=1, keepdims=True)
            packs[half, d] = jnp.where(slot == column, 1.0, 0.0).astype(bf16)


    for copy in w_copies:
        copy.wait()
    parts = [lse0_ref[0]] + [lse_in[d] for d in range(CHIPS - 1)]
    top = functools.reduce(jnp.maximum, parts)
    weights = [jnp.exp2(part - top) for part in parts]
    total = functools.reduce(jnp.add, weights)
    for d in range(CHIPS):
        column = jnp.transpose(weights[d] / total)
        for g in range(CHUNK // HD):
            mixing[d, g * HD : (g + 1) * HD] = jnp.broadcast_to(column[:, g : g + 1], (HD, HD))
    a_copies = []
    for k in range(SIDE):
        for d in (1, 3, 2):
            x_copies[k, d].wait()
        for i in range(SIDE):
            to = lax.rem(yy + k, SIDE) * SIDE + lax.rem(zz + i, SIDE)
            rows = pl.ds(pl.multiple_of(to * TOK, TOK), TOK)
            mixed = mixing[0, rows, :] * o0_ref[0, rows, :].astype(jnp.float32)
            for d in range(CHIPS - 1):
                mixed += mixing[d + 1, rows, :] * o_in[d, rows, :].astype(jnp.float32)
            if k == 0 and i == 0:
                heads[me] = mixed.astype(bf16)
            else:
                n = k * SIDE + i - 1
                att[to] = mixed.astype(bf16)
                a_copies.append(
                    remote(att.at[to], heads.at[me], a_send.at[n], a_recv.at[n], (ctx, to))
                )
        if k == 0:
            for copy in i_copies:
                copy.wait()
        if k < 2:
            pack(k)

    loads[0].wait()
    for copy in a_copies:
        copy.wait()
    joined = jnp.concatenate([heads[h] for h in range(EXPERTS)], axis=1)

    @pl.loop(0, width // STEP)
    def _(c):
        cols = pl.ds(pl.multiple_of(c * STEP, STEP), STEP)
        wide[:, cols] = hid_ref[:, cols].astype(jnp.float32) + mm(joined, proj[:, cols])

    residual = wide[...].astype(bf16).astype(jnp.float32)
    wide[...] = residual
    square = jnp.mean(residual * residual, axis=1, keepdims=True)
    normed = (residual * lax.rsqrt(square + NORM_EPS) * gain_ref[...]).astype(bf16)

    l_copies = {}
    for part in range(PARTS):
        for half in range(2):
            start = half * HALF + part * PART
            line[half, part, at_first[half]] = normed[:, start : start + PART]
            view = line.at[half, part, at_first[half]]
            for d in (2, 1, 3):
                l_copies[half, part, d] = remote(
                    view, view, l_send.at[half, part, d - 1], l_recv.at[half, part, d - 1],
                    (ctx, along(firsts[half], d)),
                )
    affinity = jax.nn.sigmoid(nt(normed, router_ref[...]))
    expert_lane = lax.broadcasted_iota(jnp.int32, affinity.shape, 1)
    chosen = functools.reduce(
        jnp.logical_or, [own_ids[:, j : j + 1] == expert_lane for j in range(6)]
    )
    picked = jnp.where(chosen, affinity, 0.0)
    mix = ROUTE_SCALE * picked / jnp.sum(picked, axis=1, keepdims=True)
    for half in range(2):
        mixes[half, at_first[half]] = jnp.zeros((TOK, HD), jnp.float32)
        mixes[half, at_first[half], :, :EXPERTS] = mix
    p_copies = {}
    for part in range(PARTS):
        for half in range(2):
            for d in (1, 3, 2):
                l_copies[half, part, d].wait_recv()
            mine = pl.ds(pl.multiple_of(at_second[half] * PACK, PACK), PACK)
            tokens = jnp.concatenate([line[half, part, i] for i in range(SIDE)], axis=0)
            for d in (2, 1, 3, 0):
                expert = along(seconds[half], d)
                row = place_t[half, pl.ds(expert, 1), :]
                rows = mm(jnp.where(slot_t == row, 1.0, 0.0).astype(bf16), tokens).astype(bf16)
                if d == 0:
                    pick_in[half, part, mine, :] = rows
                else:
                    pick_out[half, part, d - 1] = rows
                    p_copies[half, part, d] = remote(
                        pick_out.at[half, part, d - 1], pick_in.at[half, part, mine],
                        p_send.at[half, part, d - 1], p_recv.at[half, part, d - 1], (ctx, expert),
                    )
    m_copies = []
    for half in range(2):
        for d in (2, 1, 3):
            view = mixes.at[half, at_first[half]]
            m_copies.append(
                remote(
                    view, view, m_send.at[half, d - 1], m_recv.at[half, d - 1],
                    (ctx, along(firsts[half], d)),
                )
            )
    loads[1].wait()
    loads[2].wait()
    units = gate.shape[1]
    for part in range(PARTS):
        for half in (1, 0):
            for d in (1, 3, 2):
                p_copies[half, part, d].wait_recv()
            if half == 1:
                x_turned[...] = mm(turn[...], pick_in[1, part]).astype(bf16)
        low = pl.ds(part * PART, PART)
        high = pl.ds(HALF + part * PART, PART)
        for start in range(0, units, STEP):
            cols = slice(start, min(start + STEP, units))
            gated = mm(pick_in[0, part], gate[low, cols]) + mm(x_turned[...], gate[high, cols])
            raised = mm(pick_in[0, part], up[low, cols]) + mm(x_turned[...], up[high, cols])
            if part > 0:
                gated += sums[0, :, cols]
                raised += sums[1, :, cols]
            if part < PARTS - 1:
                sums[0, :, cols] = gated
                sums[1, :, cols] = raised
            else:
                inner[:, cols] = (gated / (1.0 + jnp.exp(-gated)) * raised).astype(bf16)
    turned[...] = mm(turn[...], inner[...]).astype(bf16)
    loads[3].wait()
    r_copies = {}
    for part in range(BACKS):
        for half in range(2):
            rows_in = inner if half == 0 else turned

            @pl.loop(0, BACK // STEP)
            def _(c):
                cols = pl.ds(pl.multiple_of(c * STEP, STEP), STEP)
                from_cols = pl.ds(pl.multiple_of(half * HALF + part * BACK + c * STEP, STEP), STEP)
                y_out[half, part, :, cols] = mm(rows_in[...], down[:, from_cols]).astype(bf16)

            for d in (2, 1, 3):
                to = lax.rem(at_second[half] + d, SIDE)
                r_copies[half, part, 0, d] = remote(
                    y_out.at[half, part, pl.ds(pl.multiple_of(to * PACK, PACK), PACK)],
                    y_in.at[half, part, d - 1],
                    r_send.at[half, part, 0, d - 1], r_recv.at[half, part, 0, d - 1],
                    (ctx, along(seconds[half], d)),
                )

    for copy in m_copies:
        copy.wait_recv()
    for part in range(BACKS):
        for half in range(2):
            here = at_second[half]
            share_of = jnp.concatenate([mixes[half, i] for i in range(SIDE)], axis=0)
            summed = jnp.zeros((LINE, BACK), jnp.float32)
            for d in (0, 1, 3, 2):
                back = (SIDE - d) % SIDE
                expert = along(seconds[half], back)
                column = jnp.sum(jnp.where(lane == expert, share_of, 0.0), axis=1, keepdims=True)
                if d == 0:
                    rows = y_out[half, part, pl.ds(pl.multiple_of(here * PACK, PACK), PACK), :]
                else:
                    r_copies[half, part, 0, d].wait_recv()
                    rows = y_in[half, part, d - 1]
                summed += column * mm(packs[half, back][:, :PACK], rows)
            for i in range(SIDE):
                z_out[half, part, i] = summed[i * TOK : (i + 1) * TOK].astype(bf16)
            for d in (2, 1, 3):
                r_copies[half, part, 1, d] = remote(
                    z_out.at[half, part, lax.rem(at_first[half] + d, SIDE)],
                    z_in.at[half, part, d - 1],
                    r_send.at[half, part, 1, d - 1], r_recv.at[half, part, 1, d - 1],
                    (ctx, along(firsts[half], d)),
                )
    for part in range(BACKS):
        for half in range(2):
            start = half * HALF + part * BACK
            cols = slice(start, start + BACK)
            result = wide[:, cols] + z_out[half, part, at_first[half]].astype(jnp.float32)
            for d in (1, 3, 2):
                r_copies[half, part, 1, d].wait_recv()
                result += z_in[half, part, d - 1].astype(jnp.float32)
            out_ref[:, cols] = result.astype(bf16)
    for group in (l_copies, p_copies, r_copies):
        for copy in group.values():
            copy.wait_send()
    for copy in m_copies:
        copy.wait_send()


def post(o0, o, lse0, lse, hidden_in, ids_t, gain, router_t, proj, w_gate, w_up, w_down):
    width = hidden_in.shape[1]
    units = w_gate.shape[1]
    anywhere = pl.BlockSpec(memory_space=pl.ANY)
    vmem = pl.BlockSpec(memory_space=pltpu.VMEM)
    bf16 = jnp.bfloat16
    f32 = jnp.float32
    dma = pltpu.SemaphoreType.DMA
    others = SIDE - 1
    return pl.pallas_call(
        post_kernel,
        out_shape=jax.ShapeDtypeStruct((TOK, width), bf16),
        in_specs=[vmem] * 8 + [anywhere] * 4,
        out_specs=vmem,
        scratch_shapes=[
            pltpu.VMEM((CHIPS - 1, CHUNK, HD), bf16),
            pltpu.VMEM((CHIPS - 1, CHUNK // HD, HD), f32),
            pltpu.VMEM((CHIPS, CHUNK, HD), f32),
            pltpu.VMEM((EXPERTS, TOK, HD), jnp.int32),
            pltpu.VMEM((EXPERTS, TOK, HD), bf16),
            pltpu.VMEM((EXPERTS, TOK, HD), bf16),
            pltpu.VMEM((width, width), bf16),
            pltpu.VMEM((width, units), bf16),
            pltpu.VMEM((width, units), bf16),
            pltpu.VMEM((units, width), bf16),
            pltpu.VMEM((TOK, width), f32),
            pltpu.VMEM((2, SIDE, LINE, LINE), bf16),
            pltpu.VMEM((2, HD, LINE), f32),
            pltpu.VMEM((ROWS, ROWS), bf16),
            pltpu.VMEM((2, PARTS, SIDE, TOK, PART), bf16),
            pltpu.VMEM((2, SIDE, TOK, HD), f32),
            pltpu.VMEM((2, PARTS, others, PACK, PART), bf16),
            pltpu.VMEM((2, PARTS, ROWS, PART), bf16),
            pltpu.VMEM((ROWS, PART), bf16),
            pltpu.VMEM((2, ROWS, units), f32),
            pltpu.VMEM((ROWS, units), bf16),
            pltpu.VMEM((ROWS, units), bf16),
            pltpu.VMEM((2, BACKS, ROWS, BACK), bf16),
            pltpu.VMEM((2, BACKS, others, PACK, BACK), bf16),
            pltpu.VMEM((2, BACKS, SIDE, TOK, BACK), bf16),
            pltpu.VMEM((2, BACKS, others, TOK, BACK), bf16),
            dma((4,)),
            dma((CHIPS - 1,)),
            dma((CHIPS - 1,)),
            dma((SIDE, CHIPS - 1)),
            dma((SIDE, CHIPS - 1)),
            dma((EXPERTS - 1,)),
            dma((EXPERTS - 1,)),
            dma((EXPERTS - 1,)),
            dma((EXPERTS - 1,)),
            dma((2, PARTS, others)),
            dma((2, PARTS, others)),
            dma((2, others)),
            dma((2, others)),
            dma((2, PARTS, others)),
            dma((2, PARTS, others)),
            dma((2, BACKS, 2, others)),
            dma((2, BACKS, 2, others)),
        ],
        compiler_params=pltpu.CompilerParams(
            collective_id=1, has_side_effects=True, vmem_limit_bytes=62 * MIB
        ),
        name="post",
    )(o0, o, lse0, lse, hidden_in, ids_t, gain, router_t, proj, w_gate, w_up, w_down)


def local(
    hidden_in, queries, keys, values, block_choice, out_proj, norm_gain, router, expert_ids,
    w_gate, w_up, w_down,
):
    width = hidden_in.shape[1]
    proj_all = lax.all_gather(out_proj, "exp", axis=0, tiled=True)
    devices = range(2 * CHIPS)
    swap = [(i, i ^ 1) for i in devices]
    k_oth = lax.ppermute(keys, "ctx", swap)
    v_oth = lax.ppermute(values, "ctx", swap)
    q_from = [
        lax.ppermute(queries, "ctx", [(i, (i - 2 * d) % (2 * CHIPS)) for i in devices])
        for d in range(1, CHIPS)
    ]
    blocks = (keys, k_oth, values, v_oth)
    choice = block_choice.T
    o0, lse0 = attend((0,), choice, (queries,), *blocks)
    o0, *q_from = lax.optimization_barrier((o0, *q_from))
    o, lse = attend((1, 2, 3), choice, q_from, *blocks)
    return post(
        o0, o, lse0, lse, hidden_in, expert_ids.T, norm_gain.reshape(1, width), router.T,
        proj_all, w_gate[0], w_up[0], w_down[0],
    )


def solution(mesh):
    placed = (
        P(("ctx", "exp"), None),
        P("ctx", "exp"),
        P("ctx", "exp"),
        P("ctx", "exp"),
        P(),
        P("exp", None),
        P(),
        P(),
        P(("ctx", "exp"), None),
        P("exp", None, None),
        P("exp", None, None),
        P("exp", None, None),
    )
    return jax.shard_map(
        local, mesh=mesh, in_specs=placed, out_specs=P(("ctx", "exp"), None), check_vma=False
    )
```
